32 devices in a mesh: tile: 16 (over z, y, core), depth: 2 (over x).
Axes of the slice: x: 2, y: 2, z: 4, core: 2. Of those that a mesh axis runs over, the one named last changes fastest.
Arguments:
- volume: float32 [32, 16, 256, 256], P('tile', 'depth'), may hold values from 0 to 1
- transfer: float32 [16, 2, 256, 256], P('depth', None, 'tile'), may hold values from -0.9 to 0.9
- measured: float32 [32, 256, 256], P('tile'), may hold values from 0.5 to 4
- background: float32 [32, 256, 256], P('tile'), may hold values from 1 to 4
- margins: int32 [32], replicated, may hold values from 8 to 32
- phases: int32 [16], P('depth'), may hold values from 0 to 255
Outputs:
- blended: float32 [32, 16, 256, 256], P('tile', 'depth')
The draws below stay inside these ranges and needn't reach their ends.
All inputs are finite; a program needn't handle non-finite values.
Results may differ from the reference program's by a relative error of at most 0.00005.
Values sent between devices are 32-bit elements; how exact they have to be, the bound alone decides.
No kernel may reach another device: no remote copies, remote signals or barrier semaphores. Data moves between devices by JAX's collectives and lax.ppermute only.
A program may use at most 128 MiB of HBM per device.

```python
import math
import jax
import jax.numpy as jnp
from jax import lax

TILE_N = 256
INTERSECTION = 32
TILES = 32
PLANES = 16


def place_ends(values, own_key, least, largest):
    shape = values.shape
    place = [jax.random.randint(jax.random.fold_in(own_key, axis), (), 0, shape[axis]) for axis in range(len(shape))]
    values = values.at[tuple(place)].set(least)
    longest = shape.index(max(shape))
    place[longest] = (place[longest] + 1) % shape[longest]
    return values.at[tuple(place)].set(largest)


def steps_of(own_key, extent, pieces, least, high):
    factor_of, own = 1.0, jax.random.fold_in(own_key, 6)
    for axis_at, blocks in pieces:
        steps = jnp.exp(jax.random.uniform(jax.random.fold_in(own, axis_at), (blocks,), jnp.float32, least / len(pieces), high / len(pieces)))
        factor_of = factor_of * jnp.repeat(steps, extent[axis_at] // blocks).reshape([-1 if axis == axis_at else 1 for axis in range(len(extent))])
    return factor_of


def gaussian(stream_key, shape, deviation, reach, shards=(), held_as=jnp.bfloat16):
    loudness = steps_of(stream_key, shape, shards, -0.22, 0.18) if shards else 1.0
    array = jax.random.normal(stream_key, shape, jnp.float32) * deviation * loudness
    return jnp.minimum(jnp.maximum(array, -reach), reach).astype(held_as)


def setup_inputs(seed: int = 0) -> dict:
    splits = jax.random.split(jax.random.key(seed), 7)
    volume = jnp.clip(1.0 * jax.random.uniform(splits[0], (TILES, PLANES, TILE_N, TILE_N), jnp.float32) ** steps_of(splits[0], (TILES, PLANES, TILE_N, TILE_N), ((0, 16), (1, 2)), -0.2, 0.2), 0.0, 1.0)
    transfer = gaussian(splits[1], (PLANES, 2, TILE_N, TILE_N), 0.15, 0.9, ((0, 2), (2, 16)), jnp.float32)
    measured = jnp.clip(jnp.exp(math.log(4.0) - 2.0794415 * jax.random.uniform(splits[2], (TILES, TILE_N, TILE_N), jnp.float32) ** steps_of(splits[2], (TILES, TILE_N, TILE_N), ((0, 16),), -0.2, 0.2)), 0.5, 4.0)
    background = jnp.clip(jnp.exp(math.log(4.0) - 1.3862944 * jax.random.uniform(splits[3], (TILES, TILE_N, TILE_N), jnp.float32) ** steps_of(splits[3], (TILES, TILE_N, TILE_N), ((0, 16),), -0.2, 0.2)), 1.0, 4.0)
    margins = place_ends(jax.random.randint(splits[4], (TILES,), INTERSECTION // 4, INTERSECTION + 1), jax.random.fold_in(splits[4], 1), INTERSECTION // 4, INTERSECTION).astype(jnp.int32)
    phases = place_ends(jax.random.randint(splits[5], (PLANES,), 0, TILE_N), jax.random.fold_in(splits[5], 1), 0, TILE_N - 1).astype(jnp.int32)
    return dict(volume=volume, transfer=transfer, measured=measured, background=background, margins=margins, phases=phases)


floor_level = 0.5
step_gain = 2.0


def shifted_table(transfer, phases):
    side = TILE_N
    columns = jnp.arange(side, dtype=jnp.int32)
    angle = ((phases[:, None] * columns[None, :]) % side).astype(jnp.float32) * (2.0 * math.pi / side)
    rotor = jnp.cos(angle) - 1j * jnp.sin(angle)
    return (transfer[:, 0] + 1j * transfer[:, 1]) * rotor[:, None, :]


def ramp_weights(margin_values):
    width = INTERSECTION
    offsets = jnp.arange(width, dtype=jnp.float32)
    margin_float = margin_values.astype(jnp.float32)[:, None]
    return jnp.clip((offsets[None, :] + 0.5 - (width - margin_float) / 2.0) / margin_float, 0.0, 1.0)


def reference(volume, transfer, measured, background, margins, phases):
    side = TILE_N
    width = INTERSECTION
    shifted = shifted_table(transfer, phases)

    def one_tile(operands):
        volume_tile, measured_tile, background_tile = operands
        spectra = jnp.fft.fft2(volume_tile)
        spectrum = jnp.sum(spectra * shifted, axis=0)
        projection = background_tile + jnp.real(jnp.fft.ifft2(spectrum))
        ratio = measured_tile / jnp.maximum(projection, floor_level)
        ratio_spectrum = jnp.fft.fft2(ratio - 1.0)
        correction = jnp.real(jnp.fft.ifft2(jnp.conj(shifted) * ratio_spectrum[None]))
        return jnp.maximum(volume_tile * (1.0 + step_gain * correction), 0.0)

    updated = lax.map(one_tile, (volume, measured, background))
    bottoms = updated[:, :, side - width:]
    tops = updated[:, :, :width]
    next_tops = jnp.roll(tops, -1, axis=0)
    prev_bottoms = jnp.roll(bottoms, 1, axis=0)
    weight_own = ramp_weights(margins)[:, None, :, None]
    weight_prev = ramp_weights(jnp.roll(margins, 1))[:, None, :, None]
    new_bottom = (1.0 - weight_own) * bottoms + weight_own * next_tops
    new_top = (1.0 - weight_prev) * prev_bottoms + weight_prev * tops
    return jnp.concatenate([new_top, updated[:, :, width:side - width], new_bottom], axis=2)
```

```python
import functools
import math

import jax
import jax.numpy as jnp
import ml_dtypes
import numpy as np
from jax import lax
from jax.experimental import pallas as pl
from jax.experimental.pallas import tpu as pltpu
from jax.sharding import PartitionSpec as P

INTERSECTION = 32
GROUP = 4
VMEM_BYTES = 16 * 1024 * 1024

floor_level = 0.5
step_gain = 2.0
highest = lax.Precision.HIGHEST
f32 = jnp.float32
bf16 = jnp.bfloat16


def trig_table(side):
    half = side // 2
    places = np.arange(side)
    angle = (np.outer(places, np.arange(half)) % side) * (2.0 * np.pi / side)
    cosine, sine = np.cos(angle), np.sin(angle)
    sine[:, 0] = 1.0 - 2.0 * (places % 2)
    table = np.concatenate([cosine, sine], axis=1).astype(np.float32)
    high = table.astype(ml_dtypes.bfloat16)
    low = (table - high.astype(np.float32)).astype(ml_dtypes.bfloat16)
    return np.stack([high, low])


def split(values):
    high = values.astype(bf16)
    return high, (values - high.astype(f32)).astype(bf16)


def dot(a, b):
    return lax.dot_general(a, b, (((1,), (0,)), ((), ())), preferred_element_type=f32)


def right(values, table):
    high, low = split(values)
    return dot(high, table[0]) + (dot(high, table[1]) + dot(low, table[0]))


def left(table, values):
    high, low = split(values)
    return dot(table[0], high) + (dot(table[0], low) + dot(table[1], high))


def masks(shape, first):
    lane0 = lax.broadcasted_iota(jnp.int32, shape, 1) == 0
    row0 = (lax.broadcasted_iota(jnp.int32, shape, 0) == 0) if first else None
    return row0, lane0


def to_pairs(cc, cs, sc, ss, first):
    row0, lane0 = masks(cc.shape, first)
    first_real = cc - jnp.where(lane0, 0.0, ss)
    first_imag = -(sc + jnp.where(lane0, 0.0, cs))
    second_real = jnp.where(lane0, cs, cc + ss)
    second_imag = jnp.where(lane0, ss, sc - cs)
    if first:
        first_real = jnp.where(row0, cc, first_real)
        first_imag = jnp.where(row0, -cs, first_imag)
        second_real = jnp.where(row0, jnp.where(lane0, ss, sc), second_real)
        second_imag = jnp.where(row0, jnp.where(lane0, sc, -ss), second_imag)
    return first_real, first_imag, second_real, second_imag


def from_pairs(yr, yi, zr, zi, first):
    row0, lane0 = masks(yr.shape, first)
    cc = jnp.where(lane0, yr, yr + zr)
    ss = jnp.where(lane0, zi, zr - yr)
    sc = jnp.where(lane0, -yi, zi - yi)
    cs = jnp.where(lane0, zr, -(yi + zi))
    if first:
        cc = jnp.where(row0, yr, cc)
        ss = jnp.where(row0, jnp.where(lane0, zr, -zi), ss)
        sc = jnp.where(row0, jnp.where(lane0, zi, zr), sc)
        cs = jnp.where(row0, -yi, cs)
    return cc, cs, sc, ss


def corner(real_part, imag_part, first):
    if not first:
        return real_part, imag_part, real_part
    row0, lane0 = masks(real_part.shape, True)
    both = row0 & lane0
    return real_part, jnp.where(both, 0.0, imag_part), jnp.where(both, imag_part, real_part)


def bands(half):
    return ((0, 8, True), (8, half, False))


def pair_kernel(where_ref, own_ref, recv_ref, first_ref, rotor_ref, out_ref, *, parts):
    planes, _, rows, width = recv_ref.shape
    index = where_ref[0]
    upper = index >= parts // 2
    lane = lax.broadcasted_iota(jnp.int32, recv_ref.shape, 3)
    row = lax.broadcasted_iota(jnp.int32, recv_ref.shape, 2)
    own = own_ref[:, :, :, :width]
    own = jnp.where((lane == 0) & upper, own_ref[:, :, :, width:], own)
    other = jnp.where(row == 0, jnp.broadcast_to(first_ref[...], recv_ref.shape), recv_ref[...])
    total = planes * 2 * rows
    to = lax.broadcasted_iota(jnp.int32, (total, total), 0)
    at = lax.broadcasted_iota(jnp.int32, (total, total), 1)
    slot, group = to & (rows - 1), to - (to & (rows - 1))
    own_row = jnp.where(upper, rows - 1 - slot, slot)
    other_row = jnp.where(upper, slot + 1, rows - slot) & (rows - 1)
    own_place = (at == group + own_row).astype(f32)
    other_place = (at == group + other_row).astype(f32)
    lane_to = lax.broadcasted_iota(jnp.int32, (width, width), 1)
    lane_at = lax.broadcasted_iota(jnp.int32, (width, width), 0)
    turn = (lane_at == ((width - lane_to) & (width - 1))).astype(f32)
    exact = functools.partial(jnp.dot, precision=highest, preferred_element_type=f32)
    own = exact(own_place, own.reshape(total, width)).reshape(planes, 2, rows, width)
    other = exact(exact(other_place, other.reshape(total, width)), turn)
    other = other.reshape(planes, 2, rows, width)
    real_part = (own[:, 0] + other[:, 0]) * 0.5
    imag_part = (own[:, 1] - other[:, 1]) * 0.5
    cosine, sine, sign = (rotor_ref[k][:, None, :] for k in range(3))
    turned_real = real_part * cosine + imag_part * sine
    turned_imag = imag_part * cosine - real_part * sine
    lane3 = lax.broadcasted_iota(jnp.int32, real_part.shape, 2)
    row3 = lax.broadcasted_iota(jnp.int32, real_part.shape, 1)
    edge = ((index == 0) & (row3 == 0)) | ((index == parts // 2) & (row3 == rows - 1))
    edge = edge & (lane3 == 0)
    out_ref[:, 0] = jnp.where(edge, own[:, 0] * cosine, turned_real)
    out_ref[:, 1] = jnp.where(edge, other[:, 0] * (cosine * sign), turned_imag)


def spectra_kernel(volume_ref, table_ref, turned_ref, out_ref, trig_ref, *, tile):
    planes, side = volume_ref.shape[1], volume_ref.shape[-1]
    group = trig_ref.shape[0]
    half = side // 2

    def step(i, carry):
        place = i * group
        across = right(volume_ref[tile, pl.ds(place, group)].reshape(group * side, side), table_ref)
        for g in range(group):
            trig_ref[g] = left(turned_ref, across[g * side : (g + 1) * side])
            for lo, hi, first in bands(half):
                parts = to_pairs(
                    trig_ref[g, lo:hi, :half],
                    trig_ref[g, lo:hi, half:],
                    trig_ref[g, half + lo : half + hi, :half],
                    trig_ref[g, half + lo : half + hi, half:],
                    first,
                )
                for k in range(4):
                    out_ref[place + g, k, lo:hi] = parts[k]
            for k in range(2, 4):
                out_ref[place + g, k] = pltpu.roll(out_ref[place + g, k], half - 1, 0)
        return carry

    lax.fori_loop(0, planes // group, step, 0)


def place_of(where_ref, mask, parts):
    owner = where_ref[0] ^ mask
    upper = owner >= parts // 2
    return upper.astype(jnp.int32), jnp.where(upper, parts - 1 - owner, owner)


def project_kernel(where_ref, *refs, masks_in, parts, tiles):
    blocks = refs[: len(masks_in)]
    spectra = refs[len(masks_in) : len(masks_in) + tiles]
    out_ref = refs[-1]
    planes, _, rows, half = blocks[0].shape
    lane = lax.broadcasted_iota(jnp.int32, (rows, half), 1)
    row = lax.broadcasted_iota(jnp.int32, (rows, half), 0)
    for j, mask in enumerate(masks_in):
        which, place = place_of(where_ref, mask, parts)
        corner_place = jnp.where(which == 1, parts // 2 - 1, 0)
        corner_row = jnp.where(place == corner_place, jnp.where(which == 1, rows - 1, 0), -1)
        both = (row == corner_row) & (lane == 0)
        span = pl.ds(pl.multiple_of(place * rows, rows), rows)
        sums = [None] * (2 * tiles)
        for p in range(planes):
            real_part, imag_part = blocks[j][p, 0], blocks[j][p, 1]
            real_again = jnp.where(both, imag_part, real_part)
            imag_part = jnp.where(both, 0.0, imag_part)
            for t in range(tiles):
                xr = spectra[t][p, 2 * which, span]
                xi = spectra[t][p, 2 * which + 1, span]
                yr = xr * real_part - xi * imag_part
                yi = xr * imag_part + xi * real_again
                sums[2 * t] = yr if p == 0 else sums[2 * t] + yr
                sums[2 * t + 1] = yi if p == 0 else sums[2 * t + 1] + yi
        for t in range(tiles):
            for k in range(2):
                out_ref[t, j, k] = sums[2 * t + k]


def assemble_kernel(where_ref, *refs, parts):
    blocks, out_ref = refs[:-1], refs[-1]
    planes, _, rows, half = blocks[0].shape
    for mask in range(parts):
        which, place = place_of(where_ref, mask, parts)
        span = pl.ds(pl.multiple_of(place * rows, rows), rows)
        for p in range(planes):
            for k in range(2):
                out_ref[p, 2 * which + k, span] = blocks[mask][p, k]
    for p in range(planes):
        for k in range(2, 4):
            out_ref[p, k] = pltpu.roll(out_ref[p, k], 1, 0)


def store_trig(trig_ref, coefficients, lo, hi, first, scale):
    half = trig_ref.shape[0] // 2
    for k in range(4):
        value = coefficients[k]
        if scale is not None:
            value = value * scale
            if first:
                row0, lane0 = masks(value.shape, True)
                value = jnp.where(row0 & lane0, 0.5 * value, value)
        r, c = divmod(k, 2)
        trig_ref[r * half + lo : r * half + hi, c * half : (c + 1) * half] = value


def update_kernel(where_ref, *refs, chained, tile, mask_sets, parts):
    sets = len(mask_sets)
    own_sums, received_sums = refs[:sets], refs[sets : 2 * sets]
    background_ref, measured_ref, factor_ref, volume_ref, table_ref, turned_ref = refs[2 * sets : 2 * sets + 6]
    out_ref, top_ref, bottom_ref, spectrum, trig_ref, updated_ref, sems = refs[2 * sets + 6 + chained :]
    half = spectrum.shape[-1]
    side = 2 * half
    width = top_ref.shape[1]
    planes = volume_ref.shape[1]
    group = trig_ref.shape[0]

    for own, received, masks_in in zip(own_sums, received_sums, mask_sets):
        rows = own.shape[2]
        for j, mask in enumerate(masks_in):
            which, place = place_of(where_ref, mask, parts)
            span = pl.ds(pl.multiple_of(place * rows, rows), rows)
            for k in range(2):
                spectrum[2 * which + k, span] = own[j, k] + received[j, k]
    for k in range(2, 4):
        spectrum[k] = pltpu.roll(spectrum[k], 1, 0)
    for lo, hi, first in bands(half):
        coefficients = from_pairs(*(spectrum[k, lo:hi] for k in range(4)), first)
        store_trig(trig_ref.at[0], coefficients, lo, hi, first, 2.0 / float(side * side))
    image = left(table_ref, right(trig_ref[0], turned_ref))
    ratio = measured_ref[tile] / jnp.maximum(background_ref[tile] + image, floor_level)
    trig_ref[0] = left(turned_ref, right(ratio - 1.0, table_ref))
    scale = 2.0 * step_gain / float(side * side)
    for lo, hi, first in bands(half):
        pairs = to_pairs(
            trig_ref[0, lo:hi, :half],
            trig_ref[0, lo:hi, half:],
            trig_ref[0, half + lo : half + hi, :half],
            trig_ref[0, half + lo : half + hi, half:],
            first,
        )
        for k in range(4):
            value = pairs[k] * scale
            if first:
                row0, lane0 = masks(value.shape, True)
                value = jnp.where(row0 & lane0, 0.5 * value, value)
            spectrum[k, lo:hi] = value

    copies = []
    for start in range(0, planes, group):
        for g in range(group):
            for lo, hi, first in bands(half):
                pairs = []
                for which in range(2):
                    real_part, imag_part, real_again = corner(
                        factor_ref[start + g, 2 * which, lo:hi],
                        factor_ref[start + g, 2 * which + 1, lo:hi],
                        first,
                    )
                    xr = spectrum[2 * which, lo:hi]
                    xi = spectrum[2 * which + 1, lo:hi]
                    pairs.append(real_part * xr + imag_part * xi)
                    pairs.append(real_again * xi - imag_part * xr)
                store_trig(trig_ref.at[g], from_pairs(*pairs, first), lo, hi, first, None)
        across = right(trig_ref[...].reshape(group * side, side), turned_ref)
        for g in range(group):
            plane = start + g
            correction = left(table_ref, across[g * side : (g + 1) * side])
            updated = jnp.maximum(volume_ref[tile, plane] * (1.0 + correction), 0.0)
            updated_ref[plane] = updated
            copy = pltpu.make_async_copy(updated_ref.at[plane], out_ref.at[tile, plane], sems.at[plane])
            copy.start()
            copies.append(copy)
            top_ref[plane] = updated[:width]
            bottom_ref[plane] = updated[side - width :]
    for copy in copies:
        copy.wait()


def blend_kernel(*refs, tiles):
    weight_ref = refs[0]
    tops = refs[1 : 2 + tiles]
    bottoms = refs[2 + tiles : 3 + 2 * tiles]
    _, out_ref, shared, sems = refs[3 + 2 * tiles :]
    side = out_ref.shape[2]
    width = shared.shape[2]
    copies = []
    for j in range(tiles + 1):
        weight = weight_ref[j]
        weight = jnp.concatenate([weight] * (shared.shape[3] // weight.shape[1]), axis=1)
        shared[j] = (1.0 - weight) * bottoms[j][...] + weight * tops[j][...]
        if j > 0:
            copies.append((j, j - 1, side - width))
        if j < tiles:
            copies.append((j, j, 0))
    started = []
    for k, (j, tile, row) in enumerate(copies):
        copy = pltpu.make_async_copy(
            shared.at[j], out_ref.at[tile, :, pl.ds(row, width), :], sems.at[k]
        )
        copy.start()
        started.append(copy)
    for copy in started:
        copy.wait()


def vmem():
    return pl.BlockSpec(memory_space=pltpu.VMEM)


def params():
    return pltpu.CompilerParams(vmem_limit_bytes=VMEM_BYTES)


def ramp_weights(margin_values):
    width = INTERSECTION
    offsets = lax.iota(f32, width)
    margin_float = margin_values.astype(f32)[:, None]
    return jnp.clip(
        (offsets[None, :] + 0.5 - (width - margin_float) / 2.0) / margin_float, 0.0, 1.0
    )


def single_masks(parts):
    return [1 << b for b in range(1, parts.bit_length() - 1)]


def swap(x, axis, mask):
    return lax.ppermute(x, axis, [(i, i ^ mask) for i in range(lax.axis_size(axis))])


def first_round(block, parts):
    held = {0: block}
    for mask in reversed(single_masks(parts)):
        held[mask] = swap(block, "tile", mask)
    return held


def second_round(held, parts):
    singles = single_masks(parts)
    more = {}
    for mask in range(2, parts, 2):
        if mask in held:
            continue
        bits = [b for b in singles if b & mask]
        source = bits[-1] if len(bits) == 2 else bits[0]
        more[mask] = swap(held[source], "tile", mask ^ source)
    return more


def both_cores(held):
    result = dict(held)
    for mask in held:
        result[mask | 1] = swap(held[mask], "tile", 1)
    return result


def depth_sum(pieces):
    depth = lax.axis_size("depth")
    if depth & (depth - 1) or depth == 1:
        pieces = [lax.psum(piece, "depth") for piece in pieces]
        return pieces, [jnp.zeros_like(piece) for piece in pieces]
    received, mask = None, 1
    while mask < depth:
        if received is not None:
            pieces = [piece + other for piece, other in zip(pieces, received)]
        received = [swap(piece, "depth", mask) for piece in pieces]
        mask *= 2
    return pieces, received


def on_device(volume, transfer, measured, background, margins, phases):
    tiles, planes, side = volume.shape[0], volume.shape[1], volume.shape[-1]
    half = side // 2
    rows = transfer.shape[2]
    width = INTERSECTION
    parts = lax.axis_size("tile")
    index = lax.axis_index("tile")
    where = jnp.reshape(index, (1,)).astype(jnp.int32)
    upper = index >= parts // 2
    table = jnp.asarray(trig_table(side))
    turned = jnp.asarray(np.ascontiguousarray(np.swapaxes(trig_table(side), 1, 2)))

    group = math.gcd(GROUP, planes)
    table_bytes = side * side * 8

    def spectra_of(tile, values):
        return pl.pallas_call(
            functools.partial(spectra_kernel, tile=tile),
            out_shape=jax.ShapeDtypeStruct((planes, 4, half, half), f32),
            in_specs=[vmem()] * 3,
            out_specs=vmem(),
            scratch_shapes=[pltpu.VMEM((group, side, side), f32)],
            compiler_params=params(),
            cost_estimate=pl.CostEstimate(
                flops=12 * planes * side**3, bytes_accessed=8 * planes * side**2 + table_bytes, transcendentals=0
            ),
            name=f"spectra{tile}",
        )(values, table, turned)

    lane = lax.iota(jnp.int32, half)
    lent = jnp.where((lane == 0) & upper, transfer[..., :half], transfer[..., half:])
    recv = lax.ppermute(lent, "tile", [(i, parts - 1 - i) for i in range(parts)])
    recv_first = lax.ppermute(
        lent[:, :, :1], "tile", [(i, (parts - i) % parts) for i in range(parts)]
    )
    early = [spectra_of(0, lax.optimization_barrier((volume, lent))[0])]
    column = jnp.where((lane == 0) & upper, half, lane)
    angle = (phases[:, None] * column[None, :] % side).astype(f32) * (2.0 * math.pi / side)
    sign = jnp.broadcast_to((1 - 2 * (phases & 1)).astype(f32)[:, None], angle.shape)
    rotor = jnp.stack([jnp.cos(angle), jnp.sin(angle), sign])
    recv, early[0] = lax.optimization_barrier((recv, early[0]))
    block = pl.pallas_call(
        functools.partial(pair_kernel, parts=parts),
        out_shape=jax.ShapeDtypeStruct((planes, 2, rows, half), f32),
        in_specs=[pl.BlockSpec(memory_space=pltpu.SMEM)] + [vmem()] * 4,
        out_specs=vmem(),
        compiler_params=params(),
        name="pair",
    )(where, transfer, recv, recv_first, rotor)
    held = first_round(block, parts)
    later = lax.optimization_barrier((volume, block))[0]
    spectra = early + [spectra_of(t, later) for t in range(1, tiles)]
    sources = [mask for mask in held if mask]
    tied = lax.optimization_barrier(tuple(held[mask] for mask in sources) + tuple(spectra))
    held.update(zip(sources, tied))
    spectra = list(tied[len(sources) :])
    more = second_round(held, parts)
    near, far = both_cores(held), both_cores(more)
    mask_sets = (tuple(sorted(near)), tuple(sorted(far)))

    def project(blocks, masks_in, name):
        count = len(masks_in)
        return pl.pallas_call(
            functools.partial(project_kernel, masks_in=masks_in, parts=parts, tiles=tiles),
            out_shape=jax.ShapeDtypeStruct((tiles, count, 2, rows, half), f32),
            in_specs=[pl.BlockSpec(memory_space=pltpu.SMEM)] + [vmem()] * (count + tiles),
            out_specs=vmem(),
            compiler_params=params(),
            name=name,
        )(where, *[blocks[mask] for mask in masks_in], *spectra)

    near_sum = project(near, mask_sets[0], "project_near")
    near_own, near_received = depth_sum([near_sum])
    far_masks = list(far)
    tied = lax.optimization_barrier(tuple(far[mask] for mask in far_masks) + (near_own[0],))
    far = dict(zip(far_masks, tied[:-1]))
    far_sum = project(far, mask_sets[1], "project_far")
    far_own, far_received = depth_sum([far_sum[t] for t in range(tiles)])
    blocks = {**near, **far}
    factor = pl.pallas_call(
        functools.partial(assemble_kernel, parts=parts),
        out_shape=jax.ShapeDtypeStruct((planes, 4, half, half), f32),
        in_specs=[pl.BlockSpec(memory_space=pltpu.SMEM)] + [vmem()] * parts,
        out_specs=vmem(),
        compiler_params=params(),
        name="assemble",
    )(where, *[blocks[mask] for mask in range(parts)])

    result = None
    tops, bottoms = [], []
    edge = jax.ShapeDtypeStruct((planes, width, side), f32)
    for t in range(tiles):
        chained = int(result is not None)
        sums = [near_own[0][t], far_own[t], near_received[0][t], far_received[t]]
        result, top, bottom = pl.pallas_call(
            functools.partial(update_kernel, chained=chained, tile=t, mask_sets=mask_sets, parts=parts),
            out_shape=(jax.ShapeDtypeStruct(volume.shape, f32), edge, edge),
            in_specs=[pl.BlockSpec(memory_space=pltpu.SMEM)]
            + [vmem()] * 10
            + [pl.BlockSpec(memory_space=pl.ANY)] * chained,
            out_specs=(pl.BlockSpec(memory_space=pl.ANY), vmem(), vmem()),
            scratch_shapes=[
                pltpu.VMEM((4, half, half), f32),
                pltpu.VMEM((group, side, side), f32),
                pltpu.VMEM((planes, side, side), f32),
                pltpu.SemaphoreType.DMA((planes,)),
            ],
            input_output_aliases={11: 0} if chained else {},
            compiler_params=params(),
            cost_estimate=pl.CostEstimate(
                flops=12 * planes * side**3, bytes_accessed=12 * planes * side**2, transcendentals=0
            ),
            name=f"update{t}",
        )(where, *sums, background, measured, factor, volume, table, turned, *([result] if chained else []))
        tops.append(top)
        bottoms.append(bottom)

    from_after = lax.ppermute(tops[0], "tile", [((i + 1) % parts, i) for i in range(parts)])
    from_before = lax.ppermute(bottoms[-1], "tile", [(i, (i + 1) % parts) for i in range(parts)])
    ring = jnp.concatenate([margins[margins.shape[0] - 1 :], margins], axis=0)
    around = lax.dynamic_slice_in_dim(ring, index * tiles, tiles + 1, 0)
    lanes = 128
    weights = jnp.broadcast_to(ramp_weights(around)[:, :, None], (tiles + 1, width, lanes))
    return pl.pallas_call(
        functools.partial(blend_kernel, tiles=tiles),
        out_shape=jax.ShapeDtypeStruct(volume.shape, f32),
        in_specs=[vmem()] * (3 + 2 * tiles) + [pl.BlockSpec(memory_space=pl.ANY)],
        out_specs=pl.BlockSpec(memory_space=pl.ANY),
        scratch_shapes=[
            pltpu.VMEM((tiles + 1, planes, width, side), f32),
            pltpu.SemaphoreType.DMA((2 * tiles,)),
        ],
        input_output_aliases={3 + 2 * tiles: 0},
        compiler_params=params(),
        name="blend",
    )(weights, *tops, from_after, from_before, *bottoms, result)


def solution(mesh):
    return jax.shard_map(
        on_device,
        mesh=mesh,
        in_specs=(
            P("tile", "depth", None, None),
            P("depth", None, "tile", None),
            P("tile", None, None),
            P("tile", None, None),
            P(),
            P("depth"),
        ),
        out_specs=P("tile", "depth", None, None),
        check_vma=False,
    )
```

```python
import functools
import math

import jax
import jax.numpy as jnp
import ml_dtypes
import numpy as np
from jax import lax
from jax.experimental import pallas as pl
from jax.experimental.pallas import tpu as pltpu
from jax.sharding import PartitionSpec as P

INTERSECTION = 32
GROUP = 4
SPLIT_LAST = True
LEND_COST = 8 * 10**9
VMEM_BYTES = 12 * 1024 * 1024

floor_level = 0.5
step_gain = 2.0
highest = lax.Precision.HIGHEST
f32 = jnp.float32
bf16 = jnp.bfloat16


def trig_table(side):
    half = side // 2
    places = np.arange(side)
    angle = (np.outer(places, np.arange(half)) % side) * (2.0 * np.pi / side)
    cosine, sine = np.cos(angle), np.sin(angle)
    sine[:, 0] = 1.0 - 2.0 * (places % 2)
    table = np.concatenate([cosine, sine], axis=1).astype(np.float32)
    high = table.astype(ml_dtypes.bfloat16)
    low = (table - high.astype(np.float32)).astype(ml_dtypes.bfloat16)
    return np.stack([high, low])


def split(values):
    high = values.astype(bf16)
    return high, (values - high.astype(f32)).astype(bf16)


def dot(a, b):
    return lax.dot_general(a, b, (((1,), (0,)), ((), ())), preferred_element_type=f32)


def right(values, table):
    high, low = split(values)
    return dot(high, table[0]) + (dot(high, table[1]) + dot(low, table[0]))


def left(table, values):
    high, low = split(values)
    return dot(table[0], high) + (dot(table[0], low) + dot(table[1], high))


def masks(shape, first):
    lane0 = lax.broadcasted_iota(jnp.int32, shape, 1) == 0
    row0 = (lax.broadcasted_iota(jnp.int32, shape, 0) == 0) if first else None
    return row0, lane0


def to_pairs(cc, cs, sc, ss, first):
    row0, lane0 = masks(cc.shape, first)
    first_real = cc - jnp.where(lane0, 0.0, ss)
    first_imag = -(sc + jnp.where(lane0, 0.0, cs))
    second_real = jnp.where(lane0, cs, cc + ss)
    second_imag = jnp.where(lane0, ss, sc - cs)
    if first:
        first_real = jnp.where(row0, cc, first_real)
        first_imag = jnp.where(row0, -cs, first_imag)
        second_real = jnp.where(row0, jnp.where(lane0, ss, sc), second_real)
        second_imag = jnp.where(row0, jnp.where(lane0, sc, -ss), second_imag)
    return first_real, first_imag, second_real, second_imag


def from_pairs(yr, yi, zr, zi, first):
    row0, lane0 = masks(yr.shape, first)
    cc = jnp.where(lane0, yr, yr + zr)
    ss = jnp.where(lane0, zi, zr - yr)
    sc = jnp.where(lane0, -yi, zi - yi)
    cs = jnp.where(lane0, zr, -(yi + zi))
    if first:
        cc = jnp.where(row0, yr, cc)
        ss = jnp.where(row0, jnp.where(lane0, zr, -zi), ss)
        sc = jnp.where(row0, jnp.where(lane0, zi, zr), sc)
        cs = jnp.where(row0, -yi, cs)
    return cc, cs, sc, ss


def corner(real_part, imag_part, first):
    if not first:
        return real_part, imag_part, real_part
    row0, lane0 = masks(real_part.shape, True)
    both = row0 & lane0
    return real_part, jnp.where(both, 0.0, imag_part), jnp.where(both, imag_part, real_part)


def bands(half):
    return ((0, 8, True), (8, half, False))


def lend_kernel(transfer_ref, out_ref, low_ref, sems, *, parts):
    half = out_ref.shape[-1]
    upper = lax.axis_index("tile") >= parts // 2
    high = pltpu.make_async_copy(transfer_ref.at[:, :, :, pl.ds(half, half)], out_ref, sems.at[0])
    low = pltpu.make_async_copy(transfer_ref.at[:, :, :, pl.ds(0, half)], low_ref, sems.at[1])
    high.start()
    low.start()
    high.wait()
    low.wait()
    lane = lax.broadcasted_iota(jnp.int32, out_ref.shape, 3)
    out_ref[...] = jnp.where((lane == 0) & upper, low_ref[...], out_ref[...])


def first_kernel(lent_ref, out_ref):
    out_ref[...] = lent_ref[:, :, :1]


def moved(place, values):
    place = place.astype(bf16)
    total = None
    for _ in range(3):
        part = values.astype(bf16)
        values = values - part.astype(f32)
        done = dot(place, part)
        total = done if total is None else total + done
    return total


def arrange_kernel(phases_ref, _, own_ref, out_ref, rotor_ref, *, parts):
    planes, _, rows, width = out_ref.shape
    side = 2 * width
    upper = lax.axis_index("tile") >= parts // 2
    lane = lax.broadcasted_iota(jnp.int32, out_ref.shape, 3)
    own = own_ref[:, :, :, :width]
    own = jnp.where((lane == 0) & upper, own_ref[:, :, :, width:], own)
    total = planes * 2 * rows
    to = lax.broadcasted_iota(jnp.int32, (total, total), 0)
    at = lax.broadcasted_iota(jnp.int32, (total, total), 1)
    slot = to & (rows - 1)
    place = at == to - slot + jnp.where(upper, rows - 1 - slot, slot)
    out_ref[...] = moved(place.astype(f32), own.reshape(total, width)).reshape(out_ref.shape)
    column = lax.broadcasted_iota(jnp.int32, (planes, width), 1)
    column = jnp.where((column == 0) & upper, width, column)
    step_of = lax.broadcasted_iota(jnp.int32, (planes, width), 0)
    phase = jnp.zeros((planes, width), jnp.int32)
    for p in range(planes):
        phase = jnp.where(step_of == p, phases_ref[p], phase)
    angle = ((phase * column) & (side - 1)).astype(f32) * (2.0 * math.pi / side)
    rotor_ref[0] = jnp.cos(angle)
    rotor_ref[1] = jnp.sin(angle)
    rotor_ref[2] = (1 - 2 * (phase & 1)).astype(f32)


def pair_kernel(own_ref, rotor_ref, recv_ref, first_ref, out_ref, *, parts):
    planes, _, rows, width = recv_ref.shape
    index = lax.axis_index("tile")
    upper = index >= parts // 2
    row = lax.broadcasted_iota(jnp.int32, recv_ref.shape, 2)
    other = jnp.where(row == 0, jnp.broadcast_to(first_ref[...], recv_ref.shape), recv_ref[...])
    total = planes * 2 * rows
    lane_to = lax.broadcasted_iota(jnp.int32, (width, width), 1)
    lane_at = lax.broadcasted_iota(jnp.int32, (width, width), 0)
    turn = (lane_at == ((width - lane_to) & (width - 1))).astype(f32).astype(bf16)
    to = lax.broadcasted_iota(jnp.int32, (total, total), 0)
    at = lax.broadcasted_iota(jnp.int32, (total, total), 1)
    slot = to & (rows - 1)
    place = at == to - slot + (jnp.where(upper, slot + 1, rows - slot) & (rows - 1))
    place = place.astype(f32).astype(bf16)
    values = other.reshape(total, width)
    other = None
    for _ in range(3):
        part = values.astype(bf16)
        values = values - part.astype(f32)
        turned = dot(dot(place, part).astype(bf16), turn)
        other = turned if other is None else other + turned
    other = other.reshape(planes, 2, rows, width)
    own = own_ref[...]
    real_part = (own[:, 0] + other[:, 0]) * 0.5
    imag_part = (own[:, 1] - other[:, 1]) * 0.5
    cosine, sine, sign = (rotor_ref[k][:, None, :] for k in range(3))
    turned_real = real_part * cosine + imag_part * sine
    turned_imag = imag_part * cosine - real_part * sine
    lane3 = lax.broadcasted_iota(jnp.int32, real_part.shape, 2)
    row3 = lax.broadcasted_iota(jnp.int32, real_part.shape, 1)
    edge = ((index == 0) & (row3 == 0)) | ((index == parts // 2) & (row3 == rows - 1))
    edge = edge & (lane3 == 0)
    out_ref[:, 0] = jnp.where(edge, own[:, 0] * cosine, turned_real)
    out_ref[:, 1] = jnp.where(edge, other[:, 0] * (cosine * sign), turned_imag)


def spectra_kernel(_, volume_ref, tables_ref, out_ref, trig_ref, *, tile):
    planes, side = volume_ref.shape[1], volume_ref.shape[-1]
    group = trig_ref.shape[0]
    half = side // 2
    table_ref, turned_ref = tables_ref.at[:2], tables_ref.at[2:]
    for place in range(0, planes, group):
        across = right(volume_ref[tile, place : place + group].reshape(group * side, side), table_ref)
        for g in range(group):
            trig_ref[g] = left(turned_ref, across[g * side : (g + 1) * side])
            for lo, hi, first in bands(half):
                parts = to_pairs(
                    trig_ref[g, lo:hi, :half],
                    trig_ref[g, lo:hi, half:],
                    trig_ref[g, half + lo : half + hi, :half],
                    trig_ref[g, half + lo : half + hi, half:],
                    first,
                )
                for k in range(4):
                    out_ref[place + g, k, lo:hi] = parts[k]
            for k in range(2, 4):
                out_ref[place + g, k] = pltpu.roll(out_ref[place + g, k], half - 1, 0)


def place_of(mask, parts):
    owner = lax.axis_index("tile") ^ mask
    upper = owner >= parts // 2
    return upper.astype(jnp.int32), jnp.where(upper, parts - 1 - owner, owner)


def project_kernel(*refs, masks_in, parts, tiles, apart):
    blocks = refs[: len(masks_in)]
    spectra = refs[len(masks_in) : len(masks_in) + tiles]
    outs = refs[len(masks_in) + tiles :]
    planes, _, rows, half = blocks[0].shape
    lane = lax.broadcasted_iota(jnp.int32, (rows, half), 1)
    row = lax.broadcasted_iota(jnp.int32, (rows, half), 0)
    for j, mask in enumerate(masks_in):
        which, place = place_of(mask, parts)
        corner_place = jnp.where(which == 1, parts // 2 - 1, 0)
        corner_row = jnp.where(place == corner_place, jnp.where(which == 1, rows - 1, 0), -1)
        both = (row == corner_row) & (lane == 0)
        span = pl.ds(pl.multiple_of(place * rows, rows), rows)
        sums = [None] * (2 * tiles)
        for p in range(planes):
            real_part, imag_part = blocks[j][p, 0], blocks[j][p, 1]
            real_again = jnp.where(both, imag_part, real_part)
            imag_part = jnp.where(both, 0.0, imag_part)
            for t in range(tiles):
                xr = spectra[t][p, 2 * which, span]
                xi = spectra[t][p, 2 * which + 1, span]
                yr = xr * real_part - xi * imag_part
                yi = xr * imag_part + xi * real_again
                sums[2 * t] = yr if p == 0 else sums[2 * t] + yr
                sums[2 * t + 1] = yi if p == 0 else sums[2 * t + 1] + yi
        for t in range(tiles):
            for k in range(2):
                if apart:
                    outs[t][j, k] = sums[2 * t + k]
                else:
                    outs[0][t, j, k] = sums[2 * t + k]


def assemble_kernel(margin_ref, *refs, parts, tiles):
    blocks, out_ref, weight_ref = refs[:-2], refs[-2], refs[-1]
    planes, _, rows, half = blocks[0].shape
    for mask in range(parts):
        which, place = place_of(mask, parts)
        span = pl.ds(pl.multiple_of(place * rows, rows), rows)
        for p in range(planes):
            for k in range(2):
                out_ref[p, 2 * which + k, span] = blocks[mask][p, k]
    for p in range(planes):
        for k in range(2, 4):
            out_ref[p, k] = pltpu.roll(out_ref[p, k], 1, 0)
    for j in range(tiles + 1):
        before = lax.axis_index("tile") * tiles + (j - 1)
        before = jnp.where(before < 0, before + margin_ref.shape[0], before)
        weight_ref[j] = ramp_weights(margin_ref[before].astype(f32), weight_ref.shape[1:])


def store_trig(trig_ref, coefficients, lo, hi, first, scale):
    half = trig_ref.shape[0] // 2
    for k in range(4):
        value = coefficients[k]
        if scale is not None:
            value = value * scale
            if first:
                row0, lane0 = masks(value.shape, True)
                value = jnp.where(row0 & lane0, 0.5 * value, value)
        r, c = divmod(k, 2)
        trig_ref[r * half + lo : r * half + hi, c * half : (c + 1) * half] = value


def update_kernel(*refs, tile, begin, end, mask_sets, parts):
    sets = len(mask_sets)
    ready = begin > 0
    take = 1 if ready else 2 * sets + 2
    background_ref, measured_ref = refs[2 * sets : 2 * sets + 2] if not ready else (None, None)
    own_sums, received_sums = list(refs[:sets]), list(refs[sets : 2 * sets])
    if not ready:
        own_sums[0], received_sums[0] = own_sums[0].at[tile], received_sums[0].at[tile]
    factor_ref, volume_ref, tables_ref = refs[take : take + 3]
    updated_ref, top_ref, bottom_ref, made_ref, trig_ref = refs[take + 3 :]
    table_ref, turned_ref = tables_ref.at[:2], tables_ref.at[2:]
    spectrum = refs[0] if ready else made_ref
    half = spectrum.shape[-1]
    side = 2 * half
    width = top_ref.shape[1]
    group = trig_ref.shape[0]
    if not ready:
        transform_ratio(
            own_sums, received_sums, background_ref.at[tile], measured_ref.at[tile],
            table_ref, turned_ref, spectrum, trig_ref, mask_sets, parts,
        )
    for start in range(begin, end, group):
        for g in range(group):
            for lo, hi, first in bands(half):
                pairs = []
                for which in range(2):
                    real_part, imag_part, real_again = corner(
                        factor_ref[start + g, 2 * which, lo:hi],
                        factor_ref[start + g, 2 * which + 1, lo:hi],
                        first,
                    )
                    xr = spectrum[2 * which, lo:hi]
                    xi = spectrum[2 * which + 1, lo:hi]
                    pairs.append(real_part * xr + imag_part * xi)
                    pairs.append(real_again * xi - imag_part * xr)
                store_trig(trig_ref.at[g], from_pairs(*pairs, first), lo, hi, first, None)
        across = right(trig_ref[...].reshape(group * side, side), turned_ref)
        for g in range(group):
            plane = start + g
            correction = left(table_ref, across[g * side : (g + 1) * side])
            updated = jnp.maximum(volume_ref[tile, plane] * (1.0 + correction), 0.0)
            updated_ref[plane - begin] = updated
            top_ref[plane - begin] = updated[:width]
            bottom_ref[plane - begin] = updated[side - width :]


def transform_ratio(
    own_sums, received_sums, background_ref, measured_ref, table_ref, turned_ref, spectrum, trig_ref, mask_sets, parts
):
    half = spectrum.shape[-1]
    side = 2 * half
    for own, received, masks_in in zip(own_sums, received_sums, mask_sets):
        rows = own.shape[2]
        for j, mask in enumerate(masks_in):
            which, place = place_of(mask, parts)
            span = pl.ds(pl.multiple_of(place * rows, rows), rows)
            for k in range(2):
                spectrum[2 * which + k, span] = own[j, k] + received[j, k]
    for k in range(2, 4):
        spectrum[k] = pltpu.roll(spectrum[k], 1, 0)
    for lo, hi, first in bands(half):
        coefficients = from_pairs(*(spectrum[k, lo:hi] for k in range(4)), first)
        store_trig(trig_ref.at[0], coefficients, lo, hi, first, 2.0 / float(side * side))
    image = left(table_ref, right(trig_ref[0], turned_ref))
    ratio = measured_ref[...] / jnp.maximum(background_ref[...] + image, floor_level)
    trig_ref[0] = left(turned_ref, right(ratio - 1.0, table_ref))
    scale = 2.0 * step_gain / float(side * side)
    for lo, hi, first in bands(half):
        pairs = to_pairs(
            trig_ref[0, lo:hi, :half],
            trig_ref[0, lo:hi, half:],
            trig_ref[0, half + lo : half + hi, :half],
            trig_ref[0, half + lo : half + hi, half:],
            first,
        )
        for k in range(4):
            value = pairs[k] * scale
            if first:
                row0, lane0 = masks(value.shape, True)
                value = jnp.where(row0 & lane0, 0.5 * value, value)
            spectrum[k, lo:hi] = value


def ramp_weights(margin, shape):
    offsets = lax.broadcasted_iota(jnp.int32, shape, 0).astype(f32)
    width = shape[0]
    start = jnp.full(shape, (width - margin) * 0.5, f32)
    return jnp.clip((offsets + 0.5 - start) / jnp.full(shape, margin, f32), 0.0, 1.0)


def blend_kernel(*refs, places, tiles, top_cuts, bottom_cuts, made, aliased):
    refs = list(refs)
    weight_ref = refs.pop(0)
    tops = {j: [(refs.pop(0), cut) for cut in top_cuts[j]] for j in places}
    bottoms = {j: [(refs.pop(0), cut) for cut in bottom_cuts[j]] for j in places}
    pieces = [(refs.pop(0), tile, cut) for tile, cut in made]
    out_ref, shared, sems = refs[aliased:]
    side = out_ref.shape[2]
    width = shared.shape[2]
    planes = shared.shape[1]
    started = []

    def send(source, target):
        copy = pltpu.make_async_copy(source, target, sems.at[len(started)])
        copy.start()
        started.append(copy)

    for ref, tile, (begin, end) in pieces:
        rows = pl.ds(width, side - 2 * width)
        send(ref.at[:, rows, :], out_ref.at[tile, pl.ds(begin, end - begin), rows, :])
    at = lambda sides, plane: [ref[plane - cut[0]] for ref, cut in sides if cut[0] <= plane < cut[1]][0]
    for n, j in enumerate(places):
        weight = weight_ref[j]
        for plane in range(planes):
            shared[n, plane] = (1.0 - weight) * at(bottoms[j], plane) + weight * at(tops[j], plane)
        if j > 0:
            send(shared.at[n], out_ref.at[j - 1, :, pl.ds(side - width, width), :])
        if j < tiles:
            send(shared.at[n], out_ref.at[j, :, pl.ds(0, width), :])
    for copy in started:
        copy.wait()


def vmem():
    return pl.BlockSpec(memory_space=pltpu.VMEM)


def params(limit=VMEM_BYTES):
    return pltpu.CompilerParams(vmem_limit_bytes=limit)


def single_masks(parts):
    return [1 << b for b in range(1, parts.bit_length() - 1)]


def swap(x, axis, mask):
    return lax.ppermute(x, axis, [(i, i ^ mask) for i in range(lax.axis_size(axis))])


def first_round(block, parts):
    held = {0: block}
    for mask in reversed(single_masks(parts)):
        held[mask] = swap(block, "tile", mask)
    return held


def second_round(held, parts):
    singles = single_masks(parts)
    more = {}
    for mask in range(2, parts, 2):
        if mask in held:
            continue
        bits = [b for b in singles if b & mask]
        source = bits[-1] if len(bits) == 2 else bits[0]
        more[mask] = swap(held[source], "tile", mask ^ source)
    return more


def both_cores(held):
    result = dict(held)
    for mask in held:
        result[mask | 1] = swap(held[mask], "tile", 1)
    return result


def depth_sum(pieces):
    depth = lax.axis_size("depth")
    if depth & (depth - 1) or depth == 1:
        pieces = [lax.psum(piece, "depth") for piece in pieces]
        return pieces, [jnp.zeros_like(piece) for piece in pieces]
    received, mask = None, 1
    while mask < depth:
        if received is not None:
            pieces = [piece + other for piece, other in zip(pieces, received)]
        received = [swap(piece, "depth", mask) for piece in pieces]
        mask *= 2
    return pieces, received


def on_device(volume, transfer, measured, background, margins, phases):
    tiles, planes, side = volume.shape[0], volume.shape[1], volume.shape[-1]
    half = side // 2
    rows = transfer.shape[2]
    width = INTERSECTION
    parts = lax.axis_size("tile")
    table = trig_table(side)
    constants = jnp.asarray(np.concatenate([table, np.swapaxes(table, 1, 2)]))

    group = math.gcd(GROUP, planes)

    def spectra_of(tile, after, tables):
        return pl.pallas_call(
            functools.partial(spectra_kernel, tile=tile),
            out_shape=jax.ShapeDtypeStruct((planes, 4, half, half), f32),
            in_specs=[vmem()] * 3,
            out_specs=vmem(),
            scratch_shapes=[pltpu.VMEM((group, side, side), f32)],
            compiler_params=params(),
            cost_estimate=pl.CostEstimate(
                flops=30 * planes * side**3, bytes_accessed=8 * planes * side**2, transcendentals=0
            ),
            name=f"spectra{tile}",
        )(after, volume, tables)

    tables = constants
    half_block = jax.ShapeDtypeStruct((planes, 2, rows, half), f32)
    first_row = jax.ShapeDtypeStruct((planes, 2, 1, half), f32)
    lent = pl.pallas_call(
        functools.partial(lend_kernel, parts=parts),
        out_shape=half_block,
        in_specs=[pl.BlockSpec(memory_space=pl.ANY)],
        out_specs=vmem(),
        scratch_shapes=[pltpu.VMEM((planes, 2, rows, half), f32), pltpu.SemaphoreType.DMA((2,))],
        compiler_params=params(),
        cost_estimate=pl.CostEstimate(flops=LEND_COST, bytes_accessed=8 * planes * rows * side, transcendentals=0),
        name="lend",
    )(transfer)
    recv = lax.ppermute(lent, "tile", [(i, parts - 1 - i) for i in range(parts)])
    lent_first = pl.pallas_call(
        first_kernel, out_shape=first_row, in_specs=[vmem()], out_specs=vmem(), compiler_params=params(), name="first"
    )(lent)
    recv_first = lax.ppermute(lent_first, "tile", [(i, (parts - i) % parts) for i in range(parts)])
    own, rotor = pl.pallas_call(
        functools.partial(arrange_kernel, parts=parts),
        out_shape=(half_block, jax.ShapeDtypeStruct((3, planes, half), f32)),
        in_specs=[pl.BlockSpec(memory_space=pltpu.SMEM), vmem(), vmem()],
        out_specs=(vmem(), vmem()),
        compiler_params=params(),
        name="arrange",
    )(phases, lent_first, transfer)
    early = [spectra_of(0, lent_first, tables)]
    recv, early[0], own = lax.optimization_barrier((recv, early[0], own))
    block = pl.pallas_call(
        functools.partial(pair_kernel, parts=parts),
        out_shape=half_block,
        in_specs=[vmem()] * 4,
        out_specs=vmem(),
        compiler_params=params(),
        name="pair",
    )(own, rotor, recv, recv_first)
    held = first_round(block, parts)
    spectra = early + [spectra_of(t, block, tables) for t in range(1, tiles)]
    sources = [mask for mask in held if mask]
    tied = lax.optimization_barrier(tuple(held[mask] for mask in sources) + tuple(spectra))
    held.update(zip(sources, tied))
    spectra = list(tied[len(sources) :])
    more = second_round(held, parts)
    near = both_cores(held)

    def project(blocks, masks_in, apart, name):
        count = len(masks_in)
        if apart:
            shapes = (jax.ShapeDtypeStruct((count, 2, rows, half), f32),) * tiles
        else:
            shapes = (jax.ShapeDtypeStruct((tiles, count, 2, rows, half), f32),)
        return pl.pallas_call(
            functools.partial(project_kernel, masks_in=masks_in, parts=parts, tiles=tiles, apart=apart),
            out_shape=shapes,
            in_specs=[vmem()] * (count + tiles),
            out_specs=(vmem(),) * len(shapes),
            compiler_params=params(),
            name=name,
        )(*[blocks[mask] for mask in masks_in], *spectra)

    near_masks = tuple(sorted(near))
    near_own, near_received = depth_sum(list(project(near, near_masks, False, "project_near")))
    order = list(more)
    tied = lax.optimization_barrier(tuple(more[mask] for mask in order) + (near_own[0],))
    far = both_cores(dict(zip(order, tied[:-1])))
    mask_sets = (near_masks, tuple(sorted(far)))
    far_masks = list(far)
    tied = lax.optimization_barrier(tuple(far[mask] for mask in far_masks) + (near_received[0],))
    far = dict(zip(far_masks, tied[:-1]))
    near_received = [tied[-1]]
    far_own, far_received = depth_sum(list(project(far, mask_sets[1], True, "project_far")))
    blocks = {**near, **far}
    factor, weights = pl.pallas_call(
        functools.partial(assemble_kernel, parts=parts, tiles=tiles),
        out_shape=(
            jax.ShapeDtypeStruct((planes, 4, half, half), f32),
            jax.ShapeDtypeStruct((tiles + 1, width, side), f32),
        ),
        in_specs=[pl.BlockSpec(memory_space=pltpu.SMEM)] + [vmem()] * parts,
        out_specs=(vmem(), vmem()),
        compiler_params=params(),
        name="assemble",
    )(margins, *[blocks[mask] for mask in range(parts)])

    backward = [((i + 1) % parts, i) for i in range(parts)]
    forward = [(i, (i + 1) % parts) for i in range(parts)]

    tops, bottoms = [[] for _ in range(tiles + 1)], [[] for _ in range(tiles + 1)]
    pieces = []
    for t in range(tiles):
        last = t == tiles - 1
        cuts = [0, planes // 2, planes] if last and SPLIT_LAST and planes % 2 == 0 else [0, planes]
        spectrum = None
        for begin, end in zip(cuts[:-1], cuts[1:]):
            step = math.gcd(GROUP, end - begin)
            if spectrum is None:
                inputs = [near_own[0], far_own[t], near_received[0], far_received[t], background, measured]
            else:
                inputs = [spectrum]
            inputs += [factor, volume, tables]
            edge = jax.ShapeDtypeStruct((end - begin, width, side), f32)
            updated, top, bottom, made = pl.pallas_call(
                functools.partial(update_kernel, tile=t, begin=begin, end=end, mask_sets=mask_sets, parts=parts),
                out_shape=(
                    jax.ShapeDtypeStruct((end - begin, side, side), f32), edge, edge,
                    jax.ShapeDtypeStruct((4, half, half) if spectrum is None else (8, 128), f32),
                ),
                in_specs=[vmem()] * len(inputs),
                out_specs=(vmem(),) * 4,
                scratch_shapes=[pltpu.VMEM((step, side, side), f32)],
                compiler_params=params(),
                cost_estimate=pl.CostEstimate(
                    flops=40 * (end - begin) * side**3,
                    bytes_accessed=12 * (end - begin) * side**2,
                    transcendentals=0,
                ),
                name=f"update{t}_{begin}",
            )(*inputs)
            cut = (begin, end)
            if spectrum is None:
                spectrum = made
            pieces.append((updated, t, cut))
            tops[t].append((top, cut))
            bottoms[t + 1].append((bottom, cut))
            if t == 0:
                tops[tiles].append((lax.ppermute(top, "tile", backward), cut))
            if last:
                bottoms[0].append((lax.ppermute(bottom, "tile", forward), cut))
                if end < planes:
                    tied = lax.optimization_barrier((spectrum, tops[tiles][0][0]))
                    spectrum, tops[tiles][0] = tied[0], (tied[1], tops[tiles][0][1])

    result = None
    for places in (tuple(range(1, tiles + 1)), (0,)):
        edges = [x for sides in (tops, bottoms) for j in places for x, _ in sides[j]]
        made = pieces if result is None else []
        inputs = [weights] + edges + [x for x, _, _ in made]
        aliased = int(result is not None)
        result = pl.pallas_call(
            functools.partial(
                blend_kernel,
                places=places,
                tiles=tiles,
                top_cuts={j: [cut for _, cut in tops[j]] for j in places},
                bottom_cuts={j: [cut for _, cut in bottoms[j]] for j in places},
                made=[(tile, cut) for _, tile, cut in made],
                aliased=aliased,
            ),
            out_shape=jax.ShapeDtypeStruct(volume.shape, f32),
            in_specs=[vmem()] * len(inputs) + [pl.BlockSpec(memory_space=pl.ANY)] * aliased,
            out_specs=pl.BlockSpec(memory_space=pl.ANY),
            scratch_shapes=[
                pltpu.VMEM((len(places), planes, width, side), f32),
                pltpu.SemaphoreType.DMA((2 * len(places) + len(made),)),
            ],
            input_output_aliases={len(inputs): 0} if aliased else {},
            compiler_params=params(),
            name=f"blend{places[0]}",
        )(*inputs, *([result] if aliased else []))
    return result


def solution(mesh):
    return jax.shard_map(
        on_device,
        mesh=mesh,
        in_specs=(
            P("tile", "depth", None, None),
            P("depth", None, "tile", None),
            P("tile", None, None),
            P("tile", None, None),
            P(),
            P("depth"),
        ),
        out_specs=P("tile", "depth", None, None),
        check_vma=False,
    )
```

```python
import functools
import math

import jax
import jax.numpy as jnp
import ml_dtypes
import numpy as np
from jax import lax
from jax.experimental import pallas as pl
from jax.experimental.pallas import tpu as pltpu
from jax.sharding import PartitionSpec as P

INTERSECTION = 32
GROUP = 1
TIE_TOP = True
FAR_EACH = True
LATER_COST = 40
CUTS = (6,)
TIE_FAR = False
REV2 = True
NEAR_FIRST = False
TIE_SPECTRA = True
REV1 = True
FIRST_LATE = False
LEND_COST = 8 * 10**9
VMEM_BYTES = 12 * 1024 * 1024

floor_level = 0.5
step_gain = 2.0
highest = lax.Precision.HIGHEST
f32 = jnp.float32
bf16 = jnp.bfloat16


def trig_table(side):
    half = side // 2
    places = np.arange(side)
    angle = (np.outer(places, np.arange(half)) % side) * (2.0 * np.pi / side)
    cosine, sine = np.cos(angle), np.sin(angle)
    sine[:, 0] = 1.0 - 2.0 * (places % 2)
    table = np.concatenate([cosine, sine], axis=1).astype(np.float32)
    high = table.astype(ml_dtypes.bfloat16)
    low = (table - high.astype(np.float32)).astype(ml_dtypes.bfloat16)
    return np.stack([high, low])


def split(values):
    high = values.astype(bf16)
    return high, (values - high.astype(f32)).astype(bf16)


def dot(a, b):
    return lax.dot_general(a, b, (((1,), (0,)), ((), ())), preferred_element_type=f32)


def right(values, table):
    high, low = split(values)
    return dot(high, table[0]) + (dot(high, table[1]) + dot(low, table[0]))


def left(table, values):
    high, low = split(values)
    return dot(table[0], high) + (dot(table[0], low) + dot(table[1], high))


def masks(shape, first):
    lane0 = lax.broadcasted_iota(jnp.int32, shape, 1) == 0
    row0 = (lax.broadcasted_iota(jnp.int32, shape, 0) == 0) if first else None
    return row0, lane0


def to_pairs(cc, cs, sc, ss, first):
    row0, lane0 = masks(cc.shape, first)
    first_real = cc - jnp.where(lane0, 0.0, ss)
    first_imag = -(sc + jnp.where(lane0, 0.0, cs))
    second_real = jnp.where(lane0, cs, cc + ss)
    second_imag = jnp.where(lane0, ss, sc - cs)
    if first:
        first_real = jnp.where(row0, cc, first_real)
        first_imag = jnp.where(row0, -cs, first_imag)
        second_real = jnp.where(row0, jnp.where(lane0, ss, sc), second_real)
        second_imag = jnp.where(row0, jnp.where(lane0, sc, -ss), second_imag)
    return first_real, first_imag, second_real, second_imag


def from_pairs(yr, yi, zr, zi, first):
    row0, lane0 = masks(yr.shape, first)
    cc = jnp.where(lane0, yr, yr + zr)
    ss = jnp.where(lane0, zi, zr - yr)
    sc = jnp.where(lane0, -yi, zi - yi)
    cs = jnp.where(lane0, zr, -(yi + zi))
    if first:
        cc = jnp.where(row0, yr, cc)
        ss = jnp.where(row0, jnp.where(lane0, zr, -zi), ss)
        sc = jnp.where(row0, jnp.where(lane0, zi, zr), sc)
        cs = jnp.where(row0, -yi, cs)
    return cc, cs, sc, ss


def corner(real_part, imag_part, first):
    if not first:
        return real_part, imag_part, real_part
    row0, lane0 = masks(real_part.shape, True)
    both = row0 & lane0
    return real_part, jnp.where(both, 0.0, imag_part), jnp.where(both, imag_part, real_part)


def bands(half):
    return ((0, 8, True), (8, half, False))


def lend_kernel(transfer_ref, out_ref, low_ref, sems, *, parts):
    half = out_ref.shape[-1]
    upper = lax.axis_index("tile") >= parts // 2
    high = pltpu.make_async_copy(transfer_ref.at[:, :, :, pl.ds(half, half)], out_ref, sems.at[0])
    low = pltpu.make_async_copy(transfer_ref.at[:, :, :, pl.ds(0, half)], low_ref, sems.at[1])
    high.start()
    low.start()
    high.wait()
    low.wait()
    lane = lax.broadcasted_iota(jnp.int32, out_ref.shape, 3)
    out_ref[...] = jnp.where((lane == 0) & upper, low_ref[...], out_ref[...])


def first_kernel(lent_ref, _, out_ref):
    out_ref[...] = lent_ref[:, :, :1]


def moved(place, values):
    place = place.astype(bf16)
    total = None
    for _ in range(3):
        part = values.astype(bf16)
        values = values - part.astype(f32)
        done = dot(place, part)
        total = done if total is None else total + done
    return total


def arrange_kernel(phases_ref, _, own_ref, out_ref, rotor_ref, *, parts):
    planes, _, rows, width = out_ref.shape
    side = 2 * width
    upper = lax.axis_index("tile") >= parts // 2
    lane = lax.broadcasted_iota(jnp.int32, out_ref.shape, 3)
    own = own_ref[:, :, :, :width]
    own = jnp.where((lane == 0) & upper, own_ref[:, :, :, width:], own)
    total = planes * 2 * rows
    to = lax.broadcasted_iota(jnp.int32, (total, total), 0)
    at = lax.broadcasted_iota(jnp.int32, (total, total), 1)
    slot = to & (rows - 1)
    place = at == to - slot + jnp.where(upper, rows - 1 - slot, slot)
    out_ref[...] = moved(place.astype(f32), own.reshape(total, width)).reshape(out_ref.shape)
    column = lax.broadcasted_iota(jnp.int32, (planes, width), 1)
    column = jnp.where((column == 0) & upper, width, column)
    step_of = lax.broadcasted_iota(jnp.int32, (planes, width), 0)
    phase = jnp.zeros((planes, width), jnp.int32)
    for p in range(planes):
        phase = jnp.where(step_of == p, phases_ref[p], phase)
    angle = ((phase * column) & (side - 1)).astype(f32) * (2.0 * math.pi / side)
    rotor_ref[0] = jnp.cos(angle)
    rotor_ref[1] = jnp.sin(angle)
    rotor_ref[2] = (1 - 2 * (phase & 1)).astype(f32)


def pair_kernel(own_ref, rotor_ref, recv_ref, first_ref, out_ref, *, parts):
    planes, _, rows, width = recv_ref.shape
    index = lax.axis_index("tile")
    upper = index >= parts // 2
    row = lax.broadcasted_iota(jnp.int32, recv_ref.shape, 2)
    other = jnp.where(row == 0, jnp.broadcast_to(first_ref[...], recv_ref.shape), recv_ref[...])
    total = planes * 2 * rows
    lane_to = lax.broadcasted_iota(jnp.int32, (width, width), 1)
    lane_at = lax.broadcasted_iota(jnp.int32, (width, width), 0)
    turn = (lane_at == ((width - lane_to) & (width - 1))).astype(f32).astype(bf16)
    to = lax.broadcasted_iota(jnp.int32, (total, total), 0)
    at = lax.broadcasted_iota(jnp.int32, (total, total), 1)
    slot = to & (rows - 1)
    place = at == to - slot + (jnp.where(upper, slot + 1, rows - slot) & (rows - 1))
    place = place.astype(f32).astype(bf16)
    values = other.reshape(total, width)
    other = None
    for _ in range(3):
        part = values.astype(bf16)
        values = values - part.astype(f32)
        turned = dot(dot(place, part).astype(bf16), turn)
        other = turned if other is None else other + turned
    other = other.reshape(planes, 2, rows, width)
    own = own_ref[...]
    real_part = (own[:, 0] + other[:, 0]) * 0.5
    imag_part = (own[:, 1] - other[:, 1]) * 0.5
    cosine, sine, sign = (rotor_ref[k][:, None, :] for k in range(3))
    turned_real = real_part * cosine + imag_part * sine
    turned_imag = imag_part * cosine - real_part * sine
    lane3 = lax.broadcasted_iota(jnp.int32, real_part.shape, 2)
    row3 = lax.broadcasted_iota(jnp.int32, real_part.shape, 1)
    edge = ((index == 0) & (row3 == 0)) | ((index == parts // 2) & (row3 == rows - 1))
    edge = edge & (lane3 == 0)
    out_ref[:, 0] = jnp.where(edge, own[:, 0] * cosine, turned_real)
    out_ref[:, 1] = jnp.where(edge, other[:, 0] * (cosine * sign), turned_imag)


def spectra_kernel(_, volume_ref, tables_ref, out_ref, trig_ref, *, tile):
    planes, side = volume_ref.shape[1], volume_ref.shape[-1]
    group = trig_ref.shape[0]
    half = side // 2
    table_ref, turned_ref = tables_ref.at[:2], tables_ref.at[2:]
    for place in range(0, planes, group):
        across = right(volume_ref[tile, place : place + group].reshape(group * side, side), table_ref)
        for g in range(group):
            trig_ref[g] = left(turned_ref, across[g * side : (g + 1) * side])
            for lo, hi, first in bands(half):
                parts = to_pairs(
                    trig_ref[g, lo:hi, :half],
                    trig_ref[g, lo:hi, half:],
                    trig_ref[g, half + lo : half + hi, :half],
                    trig_ref[g, half + lo : half + hi, half:],
                    first,
                )
                for k in range(4):
                    out_ref[place + g, k, lo:hi] = parts[k]
            for k in range(2, 4):
                out_ref[place + g, k] = pltpu.roll(out_ref[place + g, k], half - 1, 0)


def place_of(mask, parts):
    owner = lax.axis_index("tile") ^ mask
    upper = owner >= parts // 2
    return upper.astype(jnp.int32), jnp.where(upper, parts - 1 - owner, owner)


def project_kernel(*refs, masks_in, parts, tiles, apart):
    blocks = refs[: len(masks_in)]
    spectra = refs[len(masks_in) : len(masks_in) + tiles]
    outs = refs[len(masks_in) + tiles :]
    planes, _, rows, half = blocks[0].shape
    lane = lax.broadcasted_iota(jnp.int32, (rows, half), 1)
    row = lax.broadcasted_iota(jnp.int32, (rows, half), 0)
    for j, mask in enumerate(masks_in):
        which, place = place_of(mask, parts)
        corner_place = jnp.where(which == 1, parts // 2 - 1, 0)
        corner_row = jnp.where(place == corner_place, jnp.where(which == 1, rows - 1, 0), -1)
        both = (row == corner_row) & (lane == 0)
        span = pl.ds(pl.multiple_of(place * rows, rows), rows)
        sums = [None] * (2 * tiles)
        for p in range(planes):
            real_part, imag_part = blocks[j][p, 0], blocks[j][p, 1]
            real_again = jnp.where(both, imag_part, real_part)
            imag_part = jnp.where(both, 0.0, imag_part)
            for t in range(tiles):
                xr = spectra[t][p, 2 * which, span]
                xi = spectra[t][p, 2 * which + 1, span]
                yr = xr * real_part - xi * imag_part
                yi = xr * imag_part + xi * real_again
                sums[2 * t] = yr if p == 0 else sums[2 * t] + yr
                sums[2 * t + 1] = yi if p == 0 else sums[2 * t + 1] + yi
        for t in range(tiles):
            for k in range(2):
                if apart:
                    outs[t][j, k] = sums[2 * t + k]
                else:
                    outs[0][t, j, k] = sums[2 * t + k]


def assemble_kernel(margin_ref, *refs, parts, tiles):
    blocks, out_ref, weight_ref = refs[:-2], refs[-2], refs[-1]
    planes, _, rows, half = blocks[0].shape
    for mask in range(parts):
        which, place = place_of(mask, parts)
        span = pl.ds(pl.multiple_of(place * rows, rows), rows)
        for p in range(planes):
            for k in range(2):
                out_ref[p, 2 * which + k, span] = blocks[mask][p, k]
    for p in range(planes):
        for k in range(2, 4):
            out_ref[p, k] = pltpu.roll(out_ref[p, k], 1, 0)
    for j in range(tiles + 1):
        before = lax.axis_index("tile") * tiles + (j - 1)
        before = jnp.where(before < 0, before + margin_ref.shape[0], before)
        weight_ref[j] = ramp_weights(margin_ref[before].astype(f32), weight_ref.shape[1:])


def store_trig(trig_ref, coefficients, lo, hi, first, scale):
    half = trig_ref.shape[0] // 2
    for k in range(4):
        value = coefficients[k]
        if scale is not None:
            value = value * scale
            if first:
                row0, lane0 = masks(value.shape, True)
                value = jnp.where(row0 & lane0, 0.5 * value, value)
        r, c = divmod(k, 2)
        trig_ref[r * half + lo : r * half + hi, c * half : (c + 1) * half] = value


def update_kernel(*refs, tile, begin, end, mask_sets, parts):
    sets = len(mask_sets)
    ready = begin > 0
    take = 1 if ready else 2 * sets + 2
    background_ref, measured_ref = refs[2 * sets : 2 * sets + 2] if not ready else (None, None)
    own_sums, received_sums = list(refs[:sets]), list(refs[sets : 2 * sets])
    if not ready:
        own_sums[0], received_sums[0] = own_sums[0].at[tile], received_sums[0].at[tile]
    factor_ref, volume_ref, tables_ref = refs[take : take + 3]
    updated_ref, top_ref, bottom_ref, made_ref, trig_ref = refs[take + 3 :]
    table_ref, turned_ref = tables_ref.at[:2], tables_ref.at[2:]
    spectrum = refs[0] if ready else made_ref
    half = spectrum.shape[-1]
    side = 2 * half
    width = top_ref.shape[1]
    group = trig_ref.shape[0]
    if not ready:
        transform_ratio(
            own_sums, received_sums, background_ref.at[tile], measured_ref.at[tile],
            table_ref, turned_ref, spectrum, trig_ref, mask_sets, parts,
        )
    for start in range(begin, end, group):
        for g in range(group):
            for lo, hi, first in bands(half):
                pairs = []
                for which in range(2):
                    real_part, imag_part, real_again = corner(
                        factor_ref[start + g, 2 * which, lo:hi],
                        factor_ref[start + g, 2 * which + 1, lo:hi],
                        first,
                    )
                    xr = spectrum[2 * which, lo:hi]
                    xi = spectrum[2 * which + 1, lo:hi]
                    pairs.append(real_part * xr + imag_part * xi)
                    pairs.append(real_again * xi - imag_part * xr)
                store_trig(trig_ref.at[g], from_pairs(*pairs, first), lo, hi, first, None)
        across = right(trig_ref[...].reshape(group * side, side), turned_ref)
        for g in range(group):
            plane = start + g
            correction = left(table_ref, across[g * side : (g + 1) * side])
            updated = jnp.maximum(volume_ref[tile, plane] * (1.0 + correction), 0.0)
            updated_ref[plane - begin] = updated
            top_ref[plane - begin] = updated[:width]
            bottom_ref[plane - begin] = updated[side - width :]


def transform_ratio(
    own_sums, received_sums, background_ref, measured_ref, table_ref, turned_ref, spectrum, trig_ref, mask_sets, parts
):
    half = spectrum.shape[-1]
    side = 2 * half
    for own, received, masks_in in zip(own_sums, received_sums, mask_sets):
        rows = own.shape[2]
        for j, mask in enumerate(masks_in):
            which, place = place_of(mask, parts)
            span = pl.ds(pl.multiple_of(place * rows, rows), rows)
            for k in range(2):
                spectrum[2 * which + k, span] = own[j, k] + received[j, k]
    for k in range(2, 4):
        spectrum[k] = pltpu.roll(spectrum[k], 1, 0)
    for lo, hi, first in bands(half):
        coefficients = from_pairs(*(spectrum[k, lo:hi] for k in range(4)), first)
        store_trig(trig_ref.at[0], coefficients, lo, hi, first, 2.0 / float(side * side))
    image = left(table_ref, right(trig_ref[0], turned_ref))
    ratio = measured_ref[...] / jnp.maximum(background_ref[...] + image, floor_level)
    trig_ref[0] = left(turned_ref, right(ratio - 1.0, table_ref))
    scale = 2.0 * step_gain / float(side * side)
    for lo, hi, first in bands(half):
        pairs = to_pairs(
            trig_ref[0, lo:hi, :half],
            trig_ref[0, lo:hi, half:],
            trig_ref[0, half + lo : half + hi, :half],
            trig_ref[0, half + lo : half + hi, half:],
            first,
        )
        for k in range(4):
            value = pairs[k] * scale
            if first:
                row0, lane0 = masks(value.shape, True)
                value = jnp.where(row0 & lane0, 0.5 * value, value)
            spectrum[k, lo:hi] = value


def ramp_weights(margin, shape):
    offsets = lax.broadcasted_iota(jnp.int32, shape, 0).astype(f32)
    width = shape[0]
    start = jnp.full(shape, (width - margin) * 0.5, f32)
    return jnp.clip((offsets + 0.5 - start) / jnp.full(shape, margin, f32), 0.0, 1.0)


def blend_kernel(*refs, places, tiles, top_cuts, bottom_cuts, made, aliased):
    refs = list(refs)
    weight_ref = refs.pop(0)
    tops = {j: [(refs.pop(0), cut) for cut in top_cuts[j]] for j in places}
    bottoms = {j: [(refs.pop(0), cut) for cut in bottom_cuts[j]] for j in places}
    pieces = [(refs.pop(0), tile, cut) for tile, cut in made]
    out_ref, shared, sems = refs[aliased:]
    side = out_ref.shape[2]
    width = shared.shape[2]
    planes = shared.shape[1]
    started = []

    def send(source, target):
        copy = pltpu.make_async_copy(source, target, sems.at[len(started)])
        copy.start()
        started.append(copy)

    for ref, tile, (begin, end) in pieces:
        rows = pl.ds(width, side - 2 * width)
        send(ref.at[:, rows, :], out_ref.at[tile, pl.ds(begin, end - begin), rows, :])
    at = lambda sides, plane: [ref[plane - cut[0]] for ref, cut in sides if cut[0] <= plane < cut[1]][0]
    for n, j in enumerate(places):
        weight = weight_ref[j]
        for plane in range(planes):
            shared[n, plane] = (1.0 - weight) * at(bottoms[j], plane) + weight * at(tops[j], plane)
        if j > 0:
            send(shared.at[n], out_ref.at[j - 1, :, pl.ds(side - width, width), :])
        if j < tiles:
            send(shared.at[n], out_ref.at[j, :, pl.ds(0, width), :])
    for copy in started:
        copy.wait()


def vmem():
    return pl.BlockSpec(memory_space=pltpu.VMEM)


def params(limit=VMEM_BYTES):
    return pltpu.CompilerParams(vmem_limit_bytes=limit)


def single_masks(parts):
    return [1 << b for b in range(1, parts.bit_length() - 1)]


def swap(x, axis, mask):
    return lax.ppermute(x, axis, [(i, i ^ mask) for i in range(lax.axis_size(axis))])


def first_round(block, parts):
    held = {0: block}
    for mask in (reversed(single_masks(parts)) if REV1 else single_masks(parts)):
        held[mask] = swap(block, "tile", mask)
    return held


def second_round(held, parts):
    singles = single_masks(parts)
    more = {}
    for mask in (range(parts - 2, 0, -2) if REV2 else range(2, parts, 2)):
        if mask in held:
            continue
        bits = [b for b in singles if b & mask]
        source = bits[-1] if len(bits) == 2 else bits[0]
        more[mask] = swap(held[source], "tile", mask ^ source)
    return more


def both_cores(held):
    result = dict(held)
    for mask in held:
        result[mask | 1] = swap(held[mask], "tile", 1)
    return result


def depth_sum(pieces):
    depth = lax.axis_size("depth")
    if depth & (depth - 1) or depth == 1:
        pieces = [lax.psum(piece, "depth") for piece in pieces]
        return pieces, [jnp.zeros_like(piece) for piece in pieces]
    received, mask = None, 1
    while mask < depth:
        if received is not None:
            pieces = [piece + other for piece, other in zip(pieces, received)]
        received = [swap(piece, "depth", mask) for piece in pieces]
        mask *= 2
    return pieces, received


def on_device(volume, transfer, measured, background, margins, phases):
    tiles, planes, side = volume.shape[0], volume.shape[1], volume.shape[-1]
    half = side // 2
    rows = transfer.shape[2]
    width = INTERSECTION
    parts = lax.axis_size("tile")
    table = trig_table(side)
    constants = jnp.asarray(np.concatenate([table, np.swapaxes(table, 1, 2)]))

    group = math.gcd(GROUP, planes)

    def spectra_of(tile, after, tables):
        return pl.pallas_call(
            functools.partial(spectra_kernel, tile=tile),
            out_shape=jax.ShapeDtypeStruct((planes, 4, half, half), f32),
            in_specs=[vmem()] * 3,
            out_specs=vmem(),
            scratch_shapes=[pltpu.VMEM((group, side, side), f32)],
            compiler_params=params(),
            cost_estimate=pl.CostEstimate(
                flops=30 * planes * side**3, bytes_accessed=8 * planes * side**2, transcendentals=0
            ),
            name=f"spectra{tile}",
        )(after, volume, tables)

    tables = constants
    half_block = jax.ShapeDtypeStruct((planes, 2, rows, half), f32)
    first_row = jax.ShapeDtypeStruct((planes, 2, 1, half), f32)
    lent = pl.pallas_call(
        functools.partial(lend_kernel, parts=parts),
        out_shape=half_block,
        in_specs=[pl.BlockSpec(memory_space=pl.ANY)],
        out_specs=vmem(),
        scratch_shapes=[pltpu.VMEM((planes, 2, rows, half), f32), pltpu.SemaphoreType.DMA((2,))],
        compiler_params=params(),
        cost_estimate=pl.CostEstimate(flops=LEND_COST, bytes_accessed=8 * planes * rows * side, transcendentals=0),
        name="lend",
    )(transfer)
    recv = lax.ppermute(lent, "tile", [(i, parts - 1 - i) for i in range(parts)])
    early = [spectra_of(0, lent, tables)]
    lent_first = pl.pallas_call(
        first_kernel, out_shape=first_row, in_specs=[vmem()] * 2, out_specs=vmem(), compiler_params=params(), name="first"
    )(lent, early[0] if FIRST_LATE else lent)
    recv_first = lax.ppermute(lent_first, "tile", [(i, (parts - i) % parts) for i in range(parts)])
    own, rotor = pl.pallas_call(
        functools.partial(arrange_kernel, parts=parts),
        out_shape=(half_block, jax.ShapeDtypeStruct((3, planes, half), f32)),
        in_specs=[pl.BlockSpec(memory_space=pltpu.SMEM), vmem(), vmem()],
        out_specs=(vmem(), vmem()),
        compiler_params=params(),
        name="arrange",
    )(phases, lent_first, transfer)
    recv, early[0], own = lax.optimization_barrier((recv, early[0], own))
    block = pl.pallas_call(
        functools.partial(pair_kernel, parts=parts),
        out_shape=half_block,
        in_specs=[vmem()] * 4,
        out_specs=vmem(),
        compiler_params=params(),
        name="pair",
    )(own, rotor, recv, recv_first)
    held = first_round(block, parts)
    spectra = early + [spectra_of(t, block, tables) for t in range(1, tiles)]
    sources = [mask for mask in held if mask]
    tied = lax.optimization_barrier(tuple(held[mask] for mask in sources) + tuple(spectra))
    if TIE_SPECTRA:
        held.update(zip(sources, tied))
        spectra = list(tied[len(sources) :])
    if NEAR_FIRST:
        near = both_cores(held)
    more = second_round(held, parts)
    if not NEAR_FIRST:
        near = both_cores(held)

    def project(blocks, masks_in, apart, name):
        count = len(masks_in)
        if apart:
            shapes = (jax.ShapeDtypeStruct((count, 2, rows, half), f32),) * tiles
        else:
            shapes = (jax.ShapeDtypeStruct((tiles, count, 2, rows, half), f32),)
        return pl.pallas_call(
            functools.partial(project_kernel, masks_in=masks_in, parts=parts, tiles=tiles, apart=apart),
            out_shape=shapes,
            in_specs=[vmem()] * (count + tiles),
            out_specs=(vmem(),) * len(shapes),
            compiler_params=params(),
            name=name,
        )(*[blocks[mask] for mask in masks_in], *spectra)

    near_masks = tuple(sorted(near))
    near_own, near_received = depth_sum(list(project(near, near_masks, False, "project_near")))
    order = list(more)
    if FAR_EACH:
        tied = [lax.optimization_barrier((more[mask], near_own[0]))[0] for mask in order]
    else:
        tied = lax.optimization_barrier(tuple(more[mask] for mask in order) + (near_own[0],))[:-1]
    far = both_cores(dict(zip(order, tied)))
    mask_sets = (near_masks, tuple(sorted(far)))
    far_masks = list(far)
    tied = lax.optimization_barrier(tuple(far[mask] for mask in far_masks) + (near_received[0],))
    far = dict(zip(far_masks, tied[:-1]))
    near_received = [tied[-1]]
    blocks = {**near, **far}
    factor, weights = pl.pallas_call(
        functools.partial(assemble_kernel, parts=parts, tiles=tiles),
        out_shape=(
            jax.ShapeDtypeStruct((planes, 4, half, half), f32),
            jax.ShapeDtypeStruct((tiles + 1, width, side), f32),
        ),
        in_specs=[pl.BlockSpec(memory_space=pltpu.SMEM)] + [vmem()] * parts,
        out_specs=(vmem(), vmem()),
        compiler_params=params(),
        name="assemble",
    )(margins, *[blocks[mask] for mask in range(parts)])

    far_sums = list(project(far, mask_sets[1], True, "project_far"))
    for t in range(1, tiles):
        if TIE_FAR:
            far_sums[t] = lax.optimization_barrier((far_sums[t], weights))[0]
    far_own, far_received = depth_sum(far_sums)

    backward = [((i + 1) % parts, i) for i in range(parts)]
    forward = [(i, (i + 1) % parts) for i in range(parts)]

    tops, bottoms = [[] for _ in range(tiles + 1)], [[] for _ in range(tiles + 1)]
    pieces = []
    for t in range(tiles):
        last = t == tiles - 1
        cuts = [0, *(planes * cut // 8 for cut in CUTS), planes] if last and planes % 8 == 0 else [0, planes]
        spectrum = None
        for begin, end in zip(cuts[:-1], cuts[1:]):
            step = math.gcd(GROUP, end - begin)
            if spectrum is None:
                inputs = [near_own[0], far_own[t], near_received[0], far_received[t], background, measured]
            else:
                inputs = [spectrum]
            inputs += [factor, volume, tables]
            edge = jax.ShapeDtypeStruct((end - begin, width, side), f32)
            updated, top, bottom, made = pl.pallas_call(
                functools.partial(update_kernel, tile=t, begin=begin, end=end, mask_sets=mask_sets, parts=parts),
                out_shape=(
                    jax.ShapeDtypeStruct((end - begin, side, side), f32), edge, edge,
                    jax.ShapeDtypeStruct((4, half, half) if spectrum is None else (8, 128), f32),
                ),
                in_specs=[vmem()] * len(inputs),
                out_specs=(vmem(),) * 4,
                scratch_shapes=[pltpu.VMEM((step, side, side), f32)],
                compiler_params=params(),
                cost_estimate=pl.CostEstimate(
                    flops=(40 if t == 0 else LATER_COST) * (end - begin) * side**3,
                    bytes_accessed=(12 if t == 0 else LATER_COST) * (end - begin) * side**2,
                    transcendentals=0,
                ),
                name=f"update{t}_{begin}",
            )(*inputs)
            cut = (begin, end)
            if spectrum is None:
                spectrum = made
            pieces.append((updated, t, cut))
            tops[t].append((top, cut))
            bottoms[t + 1].append((bottom, cut))
            if t == 0:
                tops[tiles].append((lax.ppermute(top, "tile", backward), cut))
            if last:
                bottoms[0].append((lax.ppermute(bottom, "tile", forward), cut))
                if begin < cuts[-2] == end and TIE_TOP:
                    tied = lax.optimization_barrier((spectrum, tops[tiles][0][0]))
                    spectrum, tops[tiles][0] = tied[0], (tied[1], tops[tiles][0][1])

    result = None
    for places in (tuple(range(1, tiles + 1)), (0,)):
        edges = [x for sides in (tops, bottoms) for j in places for x, _ in sides[j]]
        made = pieces if result is None else []
        inputs = [weights] + edges + [x for x, _, _ in made]
        aliased = int(result is not None)
        result = pl.pallas_call(
            functools.partial(
                blend_kernel,
                places=places,
                tiles=tiles,
                top_cuts={j: [cut for _, cut in tops[j]] for j in places},
                bottom_cuts={j: [cut for _, cut in bottoms[j]] for j in places},
                made=[(tile, cut) for _, tile, cut in made],
                aliased=aliased,
            ),
            out_shape=jax.ShapeDtypeStruct(volume.shape, f32),
            in_specs=[vmem()] * len(inputs) + [pl.BlockSpec(memory_space=pl.ANY)] * aliased,
            out_specs=pl.BlockSpec(memory_space=pl.ANY),
            scratch_shapes=[
                pltpu.VMEM((len(places), planes, width, side), f32),
                pltpu.SemaphoreType.DMA((2 * len(places) + len(made),)),
            ],
            input_output_aliases={len(inputs): 0} if aliased else {},
            compiler_params=params(),
            name=f"blend{places[0]}",
        )(*inputs, *([result] if aliased else []))
    return result


def solution(mesh):
    return jax.shard_map(
        on_device,
        mesh=mesh,
        in_specs=(
            P("tile", "depth", None, None),
            P("depth", None, "tile", None),
            P("tile", None, None),
            P("tile", None, None),
            P(),
            P("depth"),
        ),
        out_specs=P("tile", "depth", None, None),
        check_vma=False,
    )
```

```python
import functools
import math

import jax
import jax.numpy as jnp
import ml_dtypes
import numpy as np
from jax import lax
from jax.experimental import pallas as pl
from jax.experimental.pallas import tpu as pltpu
from jax.sharding import PartitionSpec as P

INTERSECTION = 32
GROUP = 1
TIE_TOP = False
FAR_EACH = True
LATER_COST = 40
CUTS =(5,)
TIE_FAR = True
REV2 = True
NEAR_FIRST = False
TIE_SPECTRA = True
REV1 = True
FIRST_LATE = False
LEND_COST = 8 * 10**9
VMEM_BYTES = 12 * 1024 * 1024

floor_level = 0.5
step_gain = 2.0
highest = lax.Precision.HIGHEST
f32 = jnp.float32
bf16 = jnp.bfloat16


def trig_table(side):
    half = side // 2
    places = np.arange(side)
    angle = (np.outer(places, np.arange(half)) % side) * (2.0 * np.pi / side)
    cosine, sine = np.cos(angle), np.sin(angle)
    sine[:, 0] = 1.0 - 2.0 * (places % 2)
    table = np.concatenate([cosine, sine], axis=1).astype(np.float32)
    high = table.astype(ml_dtypes.bfloat16)
    low = (table - high.astype(np.float32)).astype(ml_dtypes.bfloat16)
    return np.stack([high, low])


def split(values):
    high = values.astype(bf16)
    return high, (values - high.astype(f32)).astype(bf16)


def dot(a, b):
    return lax.dot_general(a, b, (((1,), (0,)), ((), ())), preferred_element_type=f32)


def right(values, table):
    high, low = split(values)
    return dot(high, table[0]) + (dot(high, table[1]) + dot(low, table[0]))


def left(table, values):
    high, low = split(values)
    return dot(table[0], high) + (dot(table[0], low) + dot(table[1], high))


def masks(shape, first):
    lane0 = lax.broadcasted_iota(jnp.int32, shape, 1) == 0
    row0 = (lax.broadcasted_iota(jnp.int32, shape, 0) == 0) if first else None
    return row0, lane0


def to_pairs(cc, cs, sc, ss, first):
    row0, lane0 = masks(cc.shape, first)
    first_real = cc - jnp.where(lane0, 0.0, ss)
    first_imag = -(sc + jnp.where(lane0, 0.0, cs))
    second_real = jnp.where(lane0, cs, cc + ss)
    second_imag = jnp.where(lane0, ss, sc - cs)
    if first:
        first_real = jnp.where(row0, cc, first_real)
        first_imag = jnp.where(row0, -cs, first_imag)
        second_real = jnp.where(row0, jnp.where(lane0, ss, sc), second_real)
        second_imag = jnp.where(row0, jnp.where(lane0, sc, -ss), second_imag)
    return first_real, first_imag, second_real, second_imag


def from_pairs(yr, yi, zr, zi, first):
    row0, lane0 = masks(yr.shape, first)
    cc = jnp.where(lane0, yr, yr + zr)
    ss = jnp.where(lane0, zi, zr - yr)
    sc = jnp.where(lane0, -yi, zi - yi)
    cs = jnp.where(lane0, zr, -(yi + zi))
    if first:
        cc = jnp.where(row0, yr, cc)
        ss = jnp.where(row0, jnp.where(lane0, zr, -zi), ss)
        sc = jnp.where(row0, jnp.where(lane0, zi, zr), sc)
        cs = jnp.where(row0, -yi, cs)
    return cc, cs, sc, ss


def corner(real_part, imag_part, first):
    if not first:
        return real_part, imag_part, real_part
    row0, lane0 = masks(real_part.shape, True)
    both = row0 & lane0
    return real_part, jnp.where(both, 0.0, imag_part), jnp.where(both, imag_part, real_part)


def bands(half):
    return ((0, 8, True), (8, half, False))


def lend_kernel(transfer_ref, out_ref, low_ref, sems, *, parts):
    half = out_ref.shape[-1]
    upper = lax.axis_index("tile") >= parts // 2
    high = pltpu.make_async_copy(transfer_ref.at[:, :, :, pl.ds(half, half)], out_ref, sems.at[0])
    low = pltpu.make_async_copy(transfer_ref.at[:, :, :, pl.ds(0, half)], low_ref, sems.at[1])
    high.start()
    low.start()
    high.wait()
    low.wait()
    lane = lax.broadcasted_iota(jnp.int32, out_ref.shape, 3)
    out_ref[...] = jnp.where((lane == 0) & upper, low_ref[...], out_ref[...])


def first_kernel(lent_ref, _, out_ref):
    out_ref[...] = lent_ref[:, :, :1]


def moved(place, values):
    place = place.astype(bf16)
    total = None
    for _ in range(3):
        part = values.astype(bf16)
        values = values - part.astype(f32)
        done = dot(place, part)
        total = done if total is None else total + done
    return total


def arrange_kernel(phases_ref, _, own_ref, out_ref, rotor_ref, *, parts):
    planes, _, rows, width = out_ref.shape
    side = 2 * width
    upper = lax.axis_index("tile") >= parts // 2
    lane = lax.broadcasted_iota(jnp.int32, out_ref.shape, 3)
    own = own_ref[:, :, :, :width]
    own = jnp.where((lane == 0) & upper, own_ref[:, :, :, width:], own)
    total = planes * 2 * rows
    to = lax.broadcasted_iota(jnp.int32, (total, total), 0)
    at = lax.broadcasted_iota(jnp.int32, (total, total), 1)
    slot = to & (rows - 1)
    place = at == to - slot + jnp.where(upper, rows - 1 - slot, slot)
    out_ref[...] = moved(place.astype(f32), own.reshape(total, width)).reshape(out_ref.shape)
    column = lax.broadcasted_iota(jnp.int32, (planes, width), 1)
    column = jnp.where((column == 0) & upper, width, column)
    step_of = lax.broadcasted_iota(jnp.int32, (planes, width), 0)
    phase = jnp.zeros((planes, width), jnp.int32)
    for p in range(planes):
        phase = jnp.where(step_of == p, phases_ref[p], phase)
    angle = ((phase * column) & (side - 1)).astype(f32) * (2.0 * math.pi / side)
    rotor_ref[0] = jnp.cos(angle)
    rotor_ref[1] = jnp.sin(angle)
    rotor_ref[2] = (1 - 2 * (phase & 1)).astype(f32)


def pair_kernel(own_ref, rotor_ref, recv_ref, first_ref, out_ref, *, parts):
    planes, _, rows, width = recv_ref.shape
    index = lax.axis_index("tile")
    upper = index >= parts // 2
    row = lax.broadcasted_iota(jnp.int32, recv_ref.shape, 2)
    other = jnp.where(row == 0, jnp.broadcast_to(first_ref[...], recv_ref.shape), recv_ref[...])
    total = planes * 2 * rows
    lane_to = lax.broadcasted_iota(jnp.int32, (width, width), 1)
    lane_at = lax.broadcasted_iota(jnp.int32, (width, width), 0)
    turn = (lane_at == ((width - lane_to) & (width - 1))).astype(f32).astype(bf16)
    to = lax.broadcasted_iota(jnp.int32, (total, total), 0)
    at = lax.broadcasted_iota(jnp.int32, (total, total), 1)
    slot = to & (rows - 1)
    place = at == to - slot + (jnp.where(upper, slot + 1, rows - slot) & (rows - 1))
    place = place.astype(f32).astype(bf16)
    values = other.reshape(total, width)
    other = None
    for _ in range(3):
        part = values.astype(bf16)
        values = values - part.astype(f32)
        turned = dot(dot(place, part).astype(bf16), turn)
        other = turned if other is None else other + turned
    other = other.reshape(planes, 2, rows, width)
    own = own_ref[...]
    real_part = (own[:, 0] + other[:, 0]) * 0.5
    imag_part = (own[:, 1] - other[:, 1]) * 0.5
    cosine, sine, sign = (rotor_ref[k][:, None, :] for k in range(3))
    turned_real = real_part * cosine + imag_part * sine
    turned_imag = imag_part * cosine - real_part * sine
    lane3 = lax.broadcasted_iota(jnp.int32, real_part.shape, 2)
    row3 = lax.broadcasted_iota(jnp.int32, real_part.shape, 1)
    edge = ((index == 0) & (row3 == 0)) | ((index == parts // 2) & (row3 == rows - 1))
    edge = edge & (lane3 == 0)
    out_ref[:, 0] = jnp.where(edge, own[:, 0] * cosine, turned_real)
    out_ref[:, 1] = jnp.where(edge, other[:, 0] * (cosine * sign), turned_imag)


def spectra_kernel(_, volume_ref, tables_ref, out_ref, trig_ref, *, tile):
    planes, side = volume_ref.shape[1], volume_ref.shape[-1]
    group = trig_ref.shape[0]
    half = side // 2
    table_ref, turned_ref = tables_ref.at[:2], tables_ref.at[2:]
    for place in range(0, planes, group):
        across = right(volume_ref[tile, place : place + group].reshape(group * side, side), table_ref)
        for g in range(group):
            trig_ref[g] = left(turned_ref, across[g * side : (g + 1) * side])
            for lo, hi, first in bands(half):
                parts = to_pairs(
                    trig_ref[g, lo:hi, :half],
                    trig_ref[g, lo:hi, half:],
                    trig_ref[g, half + lo : half + hi, :half],
                    trig_ref[g, half + lo : half + hi, half:],
                    first,
                )
                for k in range(4):
                    out_ref[place + g, k, lo:hi] = parts[k]
            for k in range(2, 4):
                out_ref[place + g, k] = pltpu.roll(out_ref[place + g, k], half - 1, 0)


def place_of(mask, parts):
    owner = lax.axis_index("tile") ^ mask
    upper = owner >= parts // 2
    return upper.astype(jnp.int32), jnp.where(upper, parts - 1 - owner, owner)


def project_kernel(*refs, masks_in, parts, tiles, apart):
    blocks = refs[: len(masks_in)]
    spectra = refs[len(masks_in) : len(masks_in) + tiles]
    outs = refs[len(masks_in) + tiles :]
    planes, _, rows, half = blocks[0].shape
    lane = lax.broadcasted_iota(jnp.int32, (rows, half), 1)
    row = lax.broadcasted_iota(jnp.int32, (rows, half), 0)
    for j, mask in enumerate(masks_in):
        which, place = place_of(mask, parts)
        corner_place = jnp.where(which == 1, parts // 2 - 1, 0)
        corner_row = jnp.where(place == corner_place, jnp.where(which == 1, rows - 1, 0), -1)
        both = (row == corner_row) & (lane == 0)
        span = pl.ds(pl.multiple_of(place * rows, rows), rows)
        sums = [None] * (2 * tiles)
        for p in range(planes):
            real_part, imag_part = blocks[j][p, 0], blocks[j][p, 1]
            real_again = jnp.where(both, imag_part, real_part)
            imag_part = jnp.where(both, 0.0, imag_part)
            for t in range(tiles):
                xr = spectra[t][p, 2 * which, span]
                xi = spectra[t][p, 2 * which + 1, span]
                yr = xr * real_part - xi * imag_part
                yi = xr * imag_part + xi * real_again
                sums[2 * t] = yr if p == 0 else sums[2 * t] + yr
                sums[2 * t + 1] = yi if p == 0 else sums[2 * t + 1] + yi
        for t in range(tiles):
            for k in range(2):
                if apart:
                    outs[t][j, k] = sums[2 * t + k]
                else:
                    outs[0][t, j, k] = sums[2 * t + k]


def assemble_kernel(margin_ref, *refs, parts, tiles):
    blocks, out_ref, weight_ref = refs[:-2], refs[-2], refs[-1]
    planes, _, rows, half = blocks[0].shape
    for mask in range(parts):
        which, place = place_of(mask, parts)
        span = pl.ds(pl.multiple_of(place * rows, rows), rows)
        for p in range(planes):
            for k in range(2):
                out_ref[p, 2 * which + k, span] = blocks[mask][p, k]
    for p in range(planes):
        for k in range(2, 4):
            out_ref[p, k] = pltpu.roll(out_ref[p, k], 1, 0)
    for j in range(tiles + 1):
        before = lax.axis_index("tile") * tiles + (j - 1)
        before = jnp.where(before < 0, before + margin_ref.shape[0], before)
        weight_ref[j] = ramp_weights(margin_ref[before].astype(f32), weight_ref.shape[1:])


def store_trig(trig_ref, coefficients, lo, hi, first, scale):
    half = trig_ref.shape[0] // 2
    for k in range(4):
        value = coefficients[k]
        if scale is not None:
            value = value * scale
            if first:
                row0, lane0 = masks(value.shape, True)
                value = jnp.where(row0 & lane0, 0.5 * value, value)
        r, c = divmod(k, 2)
        trig_ref[r * half + lo : r * half + hi, c * half : (c + 1) * half] = value


def update_kernel(*refs, tile, begin, end, mask_sets, parts):
    sets = len(mask_sets)
    ready = begin > 0
    take = 1 if ready else 2 * sets + 2
    background_ref, measured_ref = refs[2 * sets : 2 * sets + 2] if not ready else (None, None)
    own_sums, received_sums = list(refs[:sets]), list(refs[sets : 2 * sets])
    if not ready:
        own_sums[0], received_sums[0] = own_sums[0].at[tile], received_sums[0].at[tile]
    factor_ref, volume_ref, tables_ref = refs[take : take + 3]
    updated_ref, top_ref, bottom_ref, made_ref, trig_ref = refs[take + 3 :]
    table_ref, turned_ref = tables_ref.at[:2], tables_ref.at[2:]
    spectrum = refs[0] if ready else made_ref
    half = spectrum.shape[-1]
    side = 2 * half
    width = top_ref.shape[1]
    group = trig_ref.shape[0]
    if not ready:
        transform_ratio(
            own_sums, received_sums, background_ref.at[tile], measured_ref.at[tile],
            table_ref, turned_ref, spectrum, trig_ref, mask_sets, parts,
        )
    for start in range(begin, end, group):
        for g in range(group):
            for lo, hi, first in bands(half):
                pairs = []
                for which in range(2):
                    real_part, imag_part, real_again = corner(
                        factor_ref[start + g, 2 * which, lo:hi],
                        factor_ref[start + g, 2 * which + 1, lo:hi],
                        first,
                    )
                    xr = spectrum[2 * which, lo:hi]
                    xi = spectrum[2 * which + 1, lo:hi]
                    pairs.append(real_part * xr + imag_part * xi)
                    pairs.append(real_again * xi - imag_part * xr)
                store_trig(trig_ref.at[g], from_pairs(*pairs, first), lo, hi, first, None)
        across = right(trig_ref[...].reshape(group * side, side), turned_ref)
        for g in range(group):
            plane = start + g
            correction = left(table_ref, across[g * side : (g + 1) * side])
            updated = jnp.maximum(volume_ref[tile, plane] * (1.0 + correction), 0.0)
            updated_ref[plane - begin] = updated
            top_ref[plane - begin] = updated[:width]
            bottom_ref[plane - begin] = updated[side - width :]


def transform_ratio(
    own_sums, received_sums, background_ref, measured_ref, table_ref, turned_ref, spectrum, trig_ref, mask_sets, parts
):
    half = spectrum.shape[-1]
    side = 2 * half
    for own, received, masks_in in zip(own_sums, received_sums, mask_sets):
        rows = own.shape[2]
        for j, mask in enumerate(masks_in):
            which, place = place_of(mask, parts)
            span = pl.ds(pl.multiple_of(place * rows, rows), rows)
            for k in range(2):
                spectrum[2 * which + k, span] = own[j, k] + received[j, k]
    for k in range(2, 4):
        spectrum[k] = pltpu.roll(spectrum[k], 1, 0)
    for lo, hi, first in bands(half):
        coefficients = from_pairs(*(spectrum[k, lo:hi] for k in range(4)), first)
        store_trig(trig_ref.at[0], coefficients, lo, hi, first, 2.0 / float(side * side))
    image = left(table_ref, right(trig_ref[0], turned_ref))
    ratio = measured_ref[...] / jnp.maximum(background_ref[...] + image, floor_level)
    trig_ref[0] = left(turned_ref, right(ratio - 1.0, table_ref))
    scale = 2.0 * step_gain / float(side * side)
    for lo, hi, first in bands(half):
        pairs = to_pairs(
            trig_ref[0, lo:hi, :half],
            trig_ref[0, lo:hi, half:],
            trig_ref[0, half + lo : half + hi, :half],
            trig_ref[0, half + lo : half + hi, half:],
            first,
        )
        for k in range(4):
            value = pairs[k] * scale
            if first:
                row0, lane0 = masks(value.shape, True)
                value = jnp.where(row0 & lane0, 0.5 * value, value)
            spectrum[k, lo:hi] = value


def ramp_weights(margin, shape):
    offsets = lax.broadcasted_iota(jnp.int32, shape, 0).astype(f32)
    width = shape[0]
    start = jnp.full(shape, (width - margin) * 0.5, f32)
    return jnp.clip((offsets + 0.5 - start) / jnp.full(shape, margin, f32), 0.0, 1.0)


def blend_kernel(*refs, places, tiles, top_cuts, bottom_cuts, made, aliased):
    refs = list(refs)
    weight_ref = refs.pop(0)
    tops = {j: [(refs.pop(0), cut) for cut in top_cuts[j]] for j in places}
    bottoms = {j: [(refs.pop(0), cut) for cut in bottom_cuts[j]] for j in places}
    pieces = [(refs.pop(0), tile, cut) for tile, cut in made]
    out_ref, shared, sems = refs[aliased:]
    side = out_ref.shape[2]
    width = shared.shape[2]
    planes = shared.shape[1]
    started = []

    def send(source, target):
        copy = pltpu.make_async_copy(source, target, sems.at[len(started)])
        copy.start()
        started.append(copy)

    for ref, tile, (begin, end) in pieces:
        rows = pl.ds(width, side - 2 * width)
        send(ref.at[:, rows, :], out_ref.at[tile, pl.ds(begin, end - begin), rows, :])
    at = lambda sides, plane: [ref[plane - cut[0]] for ref, cut in sides if cut[0] <= plane < cut[1]][0]
    for n, j in enumerate(places):
        weight = weight_ref[j]
        for plane in range(planes):
            shared[n, plane] = (1.0 - weight) * at(bottoms[j], plane) + weight * at(tops[j], plane)
        if j > 0:
            send(shared.at[n], out_ref.at[j - 1, :, pl.ds(side - width, width), :])
        if j < tiles:
            send(shared.at[n], out_ref.at[j, :, pl.ds(0, width), :])
    for copy in started:
        copy.wait()


def vmem():
    return pl.BlockSpec(memory_space=pltpu.VMEM)


def params(limit=VMEM_BYTES):
    return pltpu.CompilerParams(vmem_limit_bytes=limit)


def single_masks(parts):
    return [1 << b for b in range(1, parts.bit_length() - 1)]


def swap(x, axis, mask):
    return lax.ppermute(x, axis, [(i, i ^ mask) for i in range(lax.axis_size(axis))])


def first_round(block, parts):
    held = {0: block}
    for mask in (reversed(single_masks(parts)) if REV1 else single_masks(parts)):
        held[mask] = swap(block, "tile", mask)
    return held


def second_round(held, parts):
    singles = single_masks(parts)
    more = {}
    for mask in (range(parts - 2, 0, -2) if REV2 else range(2, parts, 2)):
        if mask in held:
            continue
        bits = [b for b in singles if b & mask]
        source = bits[-1] if len(bits) == 2 else bits[0]
        more[mask] = swap(held[source], "tile", mask ^ source)
    return more


def both_cores(held):
    result = dict(held)
    for mask in held:
        result[mask | 1] = swap(held[mask], "tile", 1)
    return result


def depth_sum(pieces):
    depth = lax.axis_size("depth")
    if depth & (depth - 1) or depth == 1:
        pieces = [lax.psum(piece, "depth") for piece in pieces]
        return pieces, [jnp.zeros_like(piece) for piece in pieces]
    received, mask = None, 1
    while mask < depth:
        if received is not None:
            pieces = [piece + other for piece, other in zip(pieces, received)]
        received = [swap(piece, "depth", mask) for piece in pieces]
        mask *= 2
    return pieces, received


def on_device(volume, transfer, measured, background, margins, phases):
    tiles, planes, side = volume.shape[0], volume.shape[1], volume.shape[-1]
    half = side // 2
    rows = transfer.shape[2]
    width = INTERSECTION
    parts = lax.axis_size("tile")
    table = trig_table(side)
    constants = jnp.asarray(np.concatenate([table, np.swapaxes(table, 1, 2)]))

    group = math.gcd(GROUP, planes)

    def spectra_of(tile, after, tables):
        return pl.pallas_call(
            functools.partial(spectra_kernel, tile=tile),
            out_shape=jax.ShapeDtypeStruct((planes, 4, half, half), f32),
            in_specs=[vmem()] * 3,
            out_specs=vmem(),
            scratch_shapes=[pltpu.VMEM((group, side, side), f32)],
            compiler_params=params(),
            cost_estimate=pl.CostEstimate(
                flops=30 * planes * side**3, bytes_accessed=8 * planes * side**2, transcendentals=0
            ),
            name=f"spectra{tile}",
        )(after, volume, tables)

    tables = constants
    half_block = jax.ShapeDtypeStruct((planes, 2, rows, half), f32)
    first_row = jax.ShapeDtypeStruct((planes, 2, 1, half), f32)
    lent = pl.pallas_call(
        functools.partial(lend_kernel, parts=parts),
        out_shape=half_block,
        in_specs=[pl.BlockSpec(memory_space=pl.ANY)],
        out_specs=vmem(),
        scratch_shapes=[pltpu.VMEM((planes, 2, rows, half), f32), pltpu.SemaphoreType.DMA((2,))],
        compiler_params=params(),
        cost_estimate=pl.CostEstimate(flops=LEND_COST, bytes_accessed=8 * planes * rows * side, transcendentals=0),
        name="lend",
    )(transfer)
    recv = lax.ppermute(lent, "tile", [(i, parts - 1 - i) for i in range(parts)])
    early = [spectra_of(0, lent, tables)]
    lent_first = pl.pallas_call(
        first_kernel, out_shape=first_row, in_specs=[vmem()] * 2, out_specs=vmem(), compiler_params=params(), name="first"
    )(lent, early[0] if FIRST_LATE else lent)
    recv_first = lax.ppermute(lent_first, "tile", [(i, (parts - i) % parts) for i in range(parts)])
    own, rotor = pl.pallas_call(
        functools.partial(arrange_kernel, parts=parts),
        out_shape=(half_block, jax.ShapeDtypeStruct((3, planes, half), f32)),
        in_specs=[pl.BlockSpec(memory_space=pltpu.SMEM), vmem(), vmem()],
        out_specs=(vmem(), vmem()),
        compiler_params=params(),
        name="arrange",
    )(phases, lent_first, transfer)
    recv, early[0], own = lax.optimization_barrier((recv, early[0], own))
    block = pl.pallas_call(
        functools.partial(pair_kernel, parts=parts),
        out_shape=half_block,
        in_specs=[vmem()] * 4,
        out_specs=vmem(),
        compiler_params=params(),
        name="pair",
    )(own, rotor, recv, recv_first)
    held = first_round(block, parts)
    spectra = early + [spectra_of(t, block, tables) for t in range(1, tiles)]
    sources = [mask for mask in held if mask]
    tied = lax.optimization_barrier(tuple(held[mask] for mask in sources) + tuple(spectra))
    if TIE_SPECTRA:
        held.update(zip(sources, tied))
        spectra = list(tied[len(sources) :])
    if NEAR_FIRST:
        near = both_cores(held)
    more = second_round(held, parts)
    if not NEAR_FIRST:
        near = both_cores(held)

    def project(blocks, masks_in, apart, name):
        count = len(masks_in)
        if apart:
            shapes = (jax.ShapeDtypeStruct((count, 2, rows, half), f32),) * tiles
        else:
            shapes = (jax.ShapeDtypeStruct((tiles, count, 2, rows, half), f32),)
        return pl.pallas_call(
            functools.partial(project_kernel, masks_in=masks_in, parts=parts, tiles=tiles, apart=apart),
            out_shape=shapes,
            in_specs=[vmem()] * (count + tiles),
            out_specs=(vmem(),) * len(shapes),
            compiler_params=params(),
            name=name,
        )(*[blocks[mask] for mask in masks_in], *spectra)

    near_masks = tuple(sorted(near))
    near_own, near_received = depth_sum(list(project(near, near_masks, False, "project_near")))
    order = list(more)
    if FAR_EACH:
        tied = [lax.optimization_barrier((more[mask], near_own[0]))[0] for mask in order]
    else:
        tied = lax.optimization_barrier(tuple(more[mask] for mask in order) + (near_own[0],))[:-1]
    far = both_cores(dict(zip(order, tied)))
    mask_sets = (near_masks, tuple(sorted(far)))
    far_masks = list(far)
    tied = lax.optimization_barrier(tuple(far[mask] for mask in far_masks) + (near_received[0],))
    far = dict(zip(far_masks, tied[:-1]))
    near_received = [tied[-1]]
    blocks = {**near, **far}
    factor, weights = pl.pallas_call(
        functools.partial(assemble_kernel, parts=parts, tiles=tiles),
        out_shape=(
            jax.ShapeDtypeStruct((planes, 4, half, half), f32),
            jax.ShapeDtypeStruct((tiles + 1, width, side), f32),
        ),
        in_specs=[pl.BlockSpec(memory_space=pltpu.SMEM)] + [vmem()] * parts,
        out_specs=(vmem(), vmem()),
        compiler_params=params(),
        name="assemble",
    )(margins, *[blocks[mask] for mask in range(parts)])

    far_sums = list(project(far, mask_sets[1], True, "project_far"))
    for t in range(1, tiles):
        if TIE_FAR:
            far_sums[t] = lax.optimization_barrier((far_sums[t], weights))[0]
    far_own, far_received = depth_sum(far_sums)

    backward = [((i + 1) % parts, i) for i in range(parts)]
    forward = [(i, (i + 1) % parts) for i in range(parts)]

    tops, bottoms = [[] for _ in range(tiles + 1)], [[] for _ in range(tiles + 1)]
    pieces = []
    for t in range(tiles):
        last = t == tiles - 1
        cuts = [0, *(planes * cut // 8 for cut in CUTS), planes] if last and planes % 8 == 0 else [0, planes]
        spectrum = None
        for begin, end in zip(cuts[:-1], cuts[1:]):
            step = math.gcd(GROUP, end - begin)
            if spectrum is None:
                inputs = [near_own[0], far_own[t], near_received[0], far_received[t], background, measured]
            else:
                inputs = [spectrum]
            inputs += [factor, volume, tables]
            edge = jax.ShapeDtypeStruct((end - begin, width, side), f32)
            updated, top, bottom, made = pl.pallas_call(
                functools.partial(update_kernel, tile=t, begin=begin, end=end, mask_sets=mask_sets, parts=parts),
                out_shape=(
                    jax.ShapeDtypeStruct((end - begin, side, side), f32), edge, edge,
                    jax.ShapeDtypeStruct((4, half, half) if spectrum is None else (8, 128), f32),
                ),
                in_specs=[vmem()] * len(inputs),
                out_specs=(vmem(),) * 4,
                scratch_shapes=[pltpu.VMEM((step, side, side), f32)],
                compiler_params=params(),
                cost_estimate=pl.CostEstimate(
                    flops=(40 if t == 0 else LATER_COST) * (end - begin) * side**3,
                    bytes_accessed=(12 if t == 0 else LATER_COST) * (end - begin) * side**2,
                    transcendentals=0,
                ),
                name=f"update{t}_{begin}",
            )(*inputs)
            cut = (begin, end)
            if spectrum is None:
                spectrum = made
            pieces.append((updated, t, cut))
            tops[t].append((top, cut))
            bottoms[t + 1].append((bottom, cut))
            if t == 0:
                tops[tiles].append((lax.ppermute(top, "tile", backward), cut))
            if last:
                bottoms[0].append((lax.ppermute(bottom, "tile", forward), cut))
                if begin < cuts[-2] == end and TIE_TOP:
                    tied = lax.optimization_barrier((spectrum, tops[tiles][0][0]))
                    spectrum, tops[tiles][0] = tied[0], (tied[1], tops[tiles][0][1])

    result = None
    for places in (tuple(range(1, tiles + 1)), (0,)):
        edges = [x for sides in (tops, bottoms) for j in places for x, _ in sides[j]]
        made = pieces if result is None else []
        inputs = [weights] + edges + [x for x, _, _ in made]
        aliased = int(result is not None)
        result = pl.pallas_call(
            functools.partial(
                blend_kernel,
                places=places,
                tiles=tiles,
                top_cuts={j: [cut for _, cut in tops[j]] for j in places},
                bottom_cuts={j: [cut for _, cut in bottoms[j]] for j in places},
                made=[(tile, cut) for _, tile, cut in made],
                aliased=aliased,
            ),
            out_shape=jax.ShapeDtypeStruct(volume.shape, f32),
            in_specs=[vmem()] * len(inputs) + [pl.BlockSpec(memory_space=pl.ANY)] * aliased,
            out_specs=pl.BlockSpec(memory_space=pl.ANY),
            scratch_shapes=[
                pltpu.VMEM((len(places), planes, width, side), f32),
                pltpu.SemaphoreType.DMA((2 * len(places) + len(made),)),
            ],
            input_output_aliases={len(inputs): 0} if aliased else {},
            compiler_params=params(),
            name=f"blend{places[0]}",
        )(*inputs, *([result] if aliased else []))
    return result


def solution(mesh):
    return jax.shard_map(
        on_device,
        mesh=mesh,
        in_specs=(
            P("tile", "depth", None, None),
            P("depth", None, "tile", None),
            P("tile", None, None),
            P("tile", None, None),
            P(),
            P("depth"),
        ),
        out_specs=P("tile", "depth", None, None),
        check_vma=False,
    )
```

```python
import functools
import math

import jax
import jax.numpy as jnp
import ml_dtypes
import numpy as np
from jax import lax
from jax.experimental import pallas as pl
from jax.experimental.pallas import tpu as pltpu
from jax.sharding import PartitionSpec as P

INTERSECTION = 32
GROUP = 1
TIE_TOP = False
FAR_EACH = True
LATER_COST = 40
CUTS =(5,)
TIE_FAR = True
REV2 = True
NEAR_FIRST = False
TIE_SPECTRA = True
REV1 = True
FIRST_LATE = False
LEND_COST = 8 * 10**9
VMEM_BYTES = 12 * 1024 * 1024

floor_level = 0.5
step_gain = 2.0
highest = lax.Precision.HIGHEST
f32 = jnp.float32
bf16 = jnp.bfloat16


def trig_table(side):
    half = side // 2
    places = np.arange(side)
    angle = (np.outer(places, np.arange(half)) % side) * (2.0 * np.pi / side)
    cosine, sine = np.cos(angle), np.sin(angle)
    sine[:, 0] = 1.0 - 2.0 * (places % 2)
    table = np.concatenate([cosine, sine], axis=1).astype(np.float32)
    high = table.astype(ml_dtypes.bfloat16)
    low = (table - high.astype(np.float32)).astype(ml_dtypes.bfloat16)
    return np.stack([high, low])


def split(values):
    high = values.astype(bf16)
    return high, (values - high.astype(f32)).astype(bf16)


def dot(a, b):
    return lax.dot_general(a, b, (((1,), (0,)), ((), ())), preferred_element_type=f32)


def right(values, table):
    high, low = split(values)
    return dot(high, table[0]) + (dot(high, table[1]) + dot(low, table[0]))


def left(table, values):
    high, low = split(values)
    side = table.shape[1]
    both = dot(table[...].reshape(2 * side, side), high)
    return both[:side] + (both[side:] + dot(table[0], low))


def masks(shape, first):
    lane0 = lax.broadcasted_iota(jnp.int32, shape, 1) == 0
    row0 = (lax.broadcasted_iota(jnp.int32, shape, 0) == 0) if first else None
    return row0, lane0


def to_pairs(cc, cs, sc, ss, first):
    row0, lane0 = masks(cc.shape, first)
    first_real = cc - jnp.where(lane0, 0.0, ss)
    first_imag = -(sc + jnp.where(lane0, 0.0, cs))
    second_real = jnp.where(lane0, cs, cc + ss)
    second_imag = jnp.where(lane0, ss, sc - cs)
    if first:
        first_real = jnp.where(row0, cc, first_real)
        first_imag = jnp.where(row0, -cs, first_imag)
        second_real = jnp.where(row0, jnp.where(lane0, ss, sc), second_real)
        second_imag = jnp.where(row0, jnp.where(lane0, sc, -ss), second_imag)
    return first_real, first_imag, second_real, second_imag


def from_pairs(yr, yi, zr, zi, first):
    row0, lane0 = masks(yr.shape, first)
    cc = jnp.where(lane0, yr, yr + zr)
    ss = jnp.where(lane0, zi, zr - yr)
    sc = jnp.where(lane0, -yi, zi - yi)
    cs = jnp.where(lane0, zr, -(yi + zi))
    if first:
        cc = jnp.where(row0, yr, cc)
        ss = jnp.where(row0, jnp.where(lane0, zr, -zi), ss)
        sc = jnp.where(row0, jnp.where(lane0, zi, zr), sc)
        cs = jnp.where(row0, -yi, cs)
    return cc, cs, sc, ss


def corner(real_part, imag_part, first):
    if not first:
        return real_part, imag_part, real_part
    row0, lane0 = masks(real_part.shape, True)
    both = row0 & lane0
    return real_part, jnp.where(both, 0.0, imag_part), jnp.where(both, imag_part, real_part)


def bands(half):
    return ((0, 8, True), (8, half, False))


def lend_kernel(transfer_ref, out_ref, low_ref, sems, *, parts):
    half = out_ref.shape[-1]
    upper = lax.axis_index("tile") >= parts // 2
    high = pltpu.make_async_copy(transfer_ref.at[:, :, :, pl.ds(half, half)], out_ref, sems.at[0])
    low = pltpu.make_async_copy(transfer_ref.at[:, :, :, pl.ds(0, half)], low_ref, sems.at[1])
    high.start()
    low.start()
    high.wait()
    low.wait()
    lane = lax.broadcasted_iota(jnp.int32, out_ref.shape, 3)
    out_ref[...] = jnp.where((lane == 0) & upper, low_ref[...], out_ref[...])


def first_kernel(lent_ref, _, out_ref):
    out_ref[...] = lent_ref[:, :, :1]


def moved(place, values):
    place = place.astype(bf16)
    total = None
    for _ in range(3):
        part = values.astype(bf16)
        values = values - part.astype(f32)
        done = dot(place, part)
        total = done if total is None else total + done
    return total


def arrange_kernel(phases_ref, _, own_ref, out_ref, rotor_ref, *, parts):
    planes, _, rows, width = out_ref.shape
    side = 2 * width
    upper = lax.axis_index("tile") >= parts // 2
    lane = lax.broadcasted_iota(jnp.int32, out_ref.shape, 3)
    own = own_ref[:, :, :, :width]
    own = jnp.where((lane == 0) & upper, own_ref[:, :, :, width:], own)
    total = planes * 2 * rows
    to = lax.broadcasted_iota(jnp.int32, (total, total), 0)
    at = lax.broadcasted_iota(jnp.int32, (total, total), 1)
    slot = to & (rows - 1)
    place = at == to - slot + jnp.where(upper, rows - 1 - slot, slot)
    out_ref[...] = moved(place.astype(f32), own.reshape(total, width)).reshape(out_ref.shape)
    column = lax.broadcasted_iota(jnp.int32, (planes, width), 1)
    column = jnp.where((column == 0) & upper, width, column)
    step_of = lax.broadcasted_iota(jnp.int32, (planes, width), 0)
    phase = jnp.zeros((planes, width), jnp.int32)
    for p in range(planes):
        phase = jnp.where(step_of == p, phases_ref[p], phase)
    angle = ((phase * column) & (side - 1)).astype(f32) * (2.0 * math.pi / side)
    rotor_ref[0] = jnp.cos(angle)
    rotor_ref[1] = jnp.sin(angle)
    rotor_ref[2] = (1 - 2 * (phase & 1)).astype(f32)


def pair_kernel(own_ref, rotor_ref, recv_ref, first_ref, out_ref, *, parts):
    planes, _, rows, width = recv_ref.shape
    index = lax.axis_index("tile")
    upper = index >= parts // 2
    row = lax.broadcasted_iota(jnp.int32, recv_ref.shape, 2)
    other = jnp.where(row == 0, jnp.broadcast_to(first_ref[...], recv_ref.shape), recv_ref[...])
    total = planes * 2 * rows
    lane_to = lax.broadcasted_iota(jnp.int32, (width, width), 1)
    lane_at = lax.broadcasted_iota(jnp.int32, (width, width), 0)
    turn = (lane_at == ((width - lane_to) & (width - 1))).astype(f32).astype(bf16)
    to = lax.broadcasted_iota(jnp.int32, (total, total), 0)
    at = lax.broadcasted_iota(jnp.int32, (total, total), 1)
    slot = to & (rows - 1)
    place = at == to - slot + (jnp.where(upper, slot + 1, rows - slot) & (rows - 1))
    place = place.astype(f32).astype(bf16)
    values = other.reshape(total, width)
    other = None
    for _ in range(3):
        part = values.astype(bf16)
        values = values - part.astype(f32)
        turned = dot(dot(place, part).astype(bf16), turn)
        other = turned if other is None else other + turned
    other = other.reshape(planes, 2, rows, width)
    own = own_ref[...]
    real_part = (own[:, 0] + other[:, 0]) * 0.5
    imag_part = (own[:, 1] - other[:, 1]) * 0.5
    cosine, sine, sign = (rotor_ref[k][:, None, :] for k in range(3))
    turned_real = real_part * cosine + imag_part * sine
    turned_imag = imag_part * cosine - real_part * sine
    lane3 = lax.broadcasted_iota(jnp.int32, real_part.shape, 2)
    row3 = lax.broadcasted_iota(jnp.int32, real_part.shape, 1)
    edge = ((index == 0) & (row3 == 0)) | ((index == parts // 2) & (row3 == rows - 1))
    edge = edge & (lane3 == 0)
    out_ref[:, 0] = jnp.where(edge, own[:, 0] * cosine, turned_real)
    out_ref[:, 1] = jnp.where(edge, other[:, 0] * (cosine * sign), turned_imag)


def spectra_kernel(_, volume_ref, tables_ref, out_ref, trig_ref, *, tile):
    planes, side = volume_ref.shape[1], volume_ref.shape[-1]
    group = trig_ref.shape[0]
    half = side // 2
    table_ref, turned_ref = tables_ref.at[:2], tables_ref.at[2:]
    for place in range(0, planes, group):
        across = right(volume_ref[tile, place : place + group].reshape(group * side, side), table_ref)
        for g in range(group):
            trig_ref[g] = left(turned_ref, across[g * side : (g + 1) * side])
            for lo, hi, first in bands(half):
                parts = to_pairs(
                    trig_ref[g, lo:hi, :half],
                    trig_ref[g, lo:hi, half:],
                    trig_ref[g, half + lo : half + hi, :half],
                    trig_ref[g, half + lo : half + hi, half:],
                    first,
                )
                for k in range(4):
                    out_ref[place + g, k, lo:hi] = parts[k]
            for k in range(2, 4):
                out_ref[place + g, k] = pltpu.roll(out_ref[place + g, k], half - 1, 0)


def place_of(mask, parts):
    owner = lax.axis_index("tile") ^ mask
    upper = owner >= parts // 2
    return upper.astype(jnp.int32), jnp.where(upper, parts - 1 - owner, owner)


def project_kernel(*refs, masks_in, parts, tiles, apart):
    blocks = refs[: len(masks_in)]
    spectra = refs[len(masks_in) : len(masks_in) + tiles]
    outs = refs[len(masks_in) + tiles :]
    planes, _, rows, half = blocks[0].shape
    lane = lax.broadcasted_iota(jnp.int32, (rows, half), 1)
    row = lax.broadcasted_iota(jnp.int32, (rows, half), 0)
    for j, mask in enumerate(masks_in):
        which, place = place_of(mask, parts)
        corner_place = jnp.where(which == 1, parts // 2 - 1, 0)
        corner_row = jnp.where(place == corner_place, jnp.where(which == 1, rows - 1, 0), -1)
        both = (row == corner_row) & (lane == 0)
        span = pl.ds(pl.multiple_of(place * rows, rows), rows)
        sums = [None] * (2 * tiles)
        for p in range(planes):
            real_part, imag_part = blocks[j][p, 0], blocks[j][p, 1]
            real_again = jnp.where(both, imag_part, real_part)
            imag_part = jnp.where(both, 0.0, imag_part)
            for t in range(tiles):
                xr = spectra[t][p, 2 * which, span]
                xi = spectra[t][p, 2 * which + 1, span]
                yr = xr * real_part - xi * imag_part
                yi = xr * imag_part + xi * real_again
                sums[2 * t] = yr if p == 0 else sums[2 * t] + yr
                sums[2 * t + 1] = yi if p == 0 else sums[2 * t + 1] + yi
        for t in range(tiles):
            for k in range(2):
                if apart:
                    outs[t][j, k] = sums[2 * t + k]
                else:
                    outs[0][t, j, k] = sums[2 * t + k]


def assemble_kernel(margin_ref, *refs, parts, tiles):
    blocks, out_ref, weight_ref = refs[:-2], refs[-2], refs[-1]
    planes, _, rows, half = blocks[0].shape
    for mask in range(parts):
        which, place = place_of(mask, parts)
        span = pl.ds(pl.multiple_of(place * rows, rows), rows)
        for p in range(planes):
            for k in range(2):
                out_ref[p, 2 * which + k, span] = blocks[mask][p, k]
    for p in range(planes):
        for k in range(2, 4):
            out_ref[p, k] = pltpu.roll(out_ref[p, k], 1, 0)
    for j in range(tiles + 1):
        before = lax.axis_index("tile") * tiles + (j - 1)
        before = jnp.where(before < 0, before + margin_ref.shape[0], before)
        weight_ref[j] = ramp_weights(margin_ref[before].astype(f32), weight_ref.shape[1:])


def store_trig(trig_ref, coefficients, lo, hi, first, scale):
    half = trig_ref.shape[0] // 2
    for k in range(4):
        value = coefficients[k]
        if scale is not None:
            value = value * scale
            if first:
                row0, lane0 = masks(value.shape, True)
                value = jnp.where(row0 & lane0, 0.5 * value, value)
        r, c = divmod(k, 2)
        trig_ref[r * half + lo : r * half + hi, c * half : (c + 1) * half] = value


def update_kernel(*refs, tile, begin, end, mask_sets, parts):
    sets = len(mask_sets)
    ready = begin > 0
    take = 1 if ready else 2 * sets + 2
    background_ref, measured_ref = refs[2 * sets : 2 * sets + 2] if not ready else (None, None)
    own_sums, received_sums = list(refs[:sets]), list(refs[sets : 2 * sets])
    if not ready:
        own_sums[0], received_sums[0] = own_sums[0].at[tile], received_sums[0].at[tile]
    factor_ref, volume_ref, tables_ref = refs[take : take + 3]
    updated_ref, top_ref, bottom_ref, made_ref, trig_ref = refs[take + 3 :]
    table_ref, turned_ref = tables_ref.at[:2], tables_ref.at[2:]
    spectrum = refs[0] if ready else made_ref
    half = spectrum.shape[-1]
    side = 2 * half
    width = top_ref.shape[1]
    group = trig_ref.shape[0]
    if not ready:
        transform_ratio(
            own_sums, received_sums, background_ref.at[tile], measured_ref.at[tile],
            table_ref, turned_ref, spectrum, trig_ref, mask_sets, parts,
        )
    for start in range(begin, end, group):
        for g in range(group):
            for lo, hi, first in bands(half):
                pairs = []
                for which in range(2):
                    real_part, imag_part, real_again = corner(
                        factor_ref[start + g, 2 * which, lo:hi],
                        factor_ref[start + g, 2 * which + 1, lo:hi],
                        first,
                    )
                    xr = spectrum[2 * which, lo:hi]
                    xi = spectrum[2 * which + 1, lo:hi]
                    pairs.append(real_part * xr + imag_part * xi)
                    pairs.append(real_again * xi - imag_part * xr)
                store_trig(trig_ref.at[g], from_pairs(*pairs, first), lo, hi, first, None)
        across = right(trig_ref[...].reshape(group * side, side), turned_ref)
        for g in range(group):
            plane = start + g
            correction = left(table_ref, across[g * side : (g + 1) * side])
            updated = jnp.maximum(volume_ref[tile, plane] * (1.0 + correction), 0.0)
            updated_ref[plane - begin] = updated
            top_ref[plane - begin] = updated[:width]
            bottom_ref[plane - begin] = updated[side - width :]


def transform_ratio(
    own_sums, received_sums, background_ref, measured_ref, table_ref, turned_ref, spectrum, trig_ref, mask_sets, parts
):
    half = spectrum.shape[-1]
    side = 2 * half
    for own, received, masks_in in zip(own_sums, received_sums, mask_sets):
        rows = own.shape[2]
        for j, mask in enumerate(masks_in):
            which, place = place_of(mask, parts)
            span = pl.ds(pl.multiple_of(place * rows, rows), rows)
            for k in range(2):
                spectrum[2 * which + k, span] = own[j, k] + received[j, k]
    for k in range(2, 4):
        spectrum[k] = pltpu.roll(spectrum[k], 1, 0)
    for lo, hi, first in bands(half):
        coefficients = from_pairs(*(spectrum[k, lo:hi] for k in range(4)), first)
        store_trig(trig_ref.at[0], coefficients, lo, hi, first, 2.0 / float(side * side))
    image = left(table_ref, right(trig_ref[0], turned_ref))
    ratio = measured_ref[...] / jnp.maximum(background_ref[...] + image, floor_level)
    trig_ref[0] = left(turned_ref, right(ratio - 1.0, table_ref))
    scale = 2.0 * step_gain / float(side * side)
    for lo, hi, first in bands(half):
        pairs = to_pairs(
            trig_ref[0, lo:hi, :half],
            trig_ref[0, lo:hi, half:],
            trig_ref[0, half + lo : half + hi, :half],
            trig_ref[0, half + lo : half + hi, half:],
            first,
        )
        for k in range(4):
            value = pairs[k] * scale
            if first:
                row0, lane0 = masks(value.shape, True)
                value = jnp.where(row0 & lane0, 0.5 * value, value)
            spectrum[k, lo:hi] = value


def ramp_weights(margin, shape):
    offsets = lax.broadcasted_iota(jnp.int32, shape, 0).astype(f32)
    width = shape[0]
    start = jnp.full(shape, (width - margin) * 0.5, f32)
    return jnp.clip((offsets + 0.5 - start) / jnp.full(shape, margin, f32), 0.0, 1.0)


def blend_kernel(*refs, places, tiles, top_cuts, bottom_cuts, made, aliased):
    refs = list(refs)
    weight_ref = refs.pop(0)
    tops = {j: [(refs.pop(0), cut) for cut in top_cuts[j]] for j in places}
    bottoms = {j: [(refs.pop(0), cut) for cut in bottom_cuts[j]] for j in places}
    pieces = [(refs.pop(0), tile, cut) for tile, cut in made]
    out_ref, shared, sems = refs[aliased:]
    side = out_ref.shape[2]
    width = shared.shape[2]
    planes = shared.shape[1]
    started = []

    def send(source, target):
        copy = pltpu.make_async_copy(source, target, sems.at[len(started)])
        copy.start()
        started.append(copy)

    for ref, tile, (begin, end) in pieces:
        rows = pl.ds(width, side - 2 * width)
        send(ref.at[:, rows, :], out_ref.at[tile, pl.ds(begin, end - begin), rows, :])
    at = lambda sides, plane: [ref[plane - cut[0]] for ref, cut in sides if cut[0] <= plane < cut[1]][0]
    for n, j in enumerate(places):
        weight = weight_ref[j]
        for plane in range(planes):
            shared[n, plane] = (1.0 - weight) * at(bottoms[j], plane) + weight * at(tops[j], plane)
        if j > 0:
            send(shared.at[n], out_ref.at[j - 1, :, pl.ds(side - width, width), :])
        if j < tiles:
            send(shared.at[n], out_ref.at[j, :, pl.ds(0, width), :])
    for copy in started:
        copy.wait()


def vmem():
    return pl.BlockSpec(memory_space=pltpu.VMEM)


def params(limit=VMEM_BYTES):
    return pltpu.CompilerParams(vmem_limit_bytes=limit)


def single_masks(parts):
    return [1 << b for b in range(1, parts.bit_length() - 1)]


def swap(x, axis, mask):
    return lax.ppermute(x, axis, [(i, i ^ mask) for i in range(lax.axis_size(axis))])


def first_round(block, parts):
    held = {0: block}
    for mask in (reversed(single_masks(parts)) if REV1 else single_masks(parts)):
        held[mask] = swap(block, "tile", mask)
    return held


def second_round(held, parts):
    singles = single_masks(parts)
    more = {}
    for mask in (range(parts - 2, 0, -2) if REV2 else range(2, parts, 2)):
        if mask in held:
            continue
        bits = [b for b in singles if b & mask]
        source = bits[-1] if len(bits) == 2 else bits[0]
        more[mask] = swap(held[source], "tile", mask ^ source)
    return more


def both_cores(held):
    result = dict(held)
    for mask in held:
        result[mask | 1] = swap(held[mask], "tile", 1)
    return result


def depth_sum(pieces):
    depth = lax.axis_size("depth")
    if depth & (depth - 1) or depth == 1:
        pieces = [lax.psum(piece, "depth") for piece in pieces]
        return pieces, [jnp.zeros_like(piece) for piece in pieces]
    received, mask = None, 1
    while mask < depth:
        if received is not None:
            pieces = [piece + other for piece, other in zip(pieces, received)]
        received = [swap(piece, "depth", mask) for piece in pieces]
        mask *= 2
    return pieces, received


def on_device(volume, transfer, measured, background, margins, phases):
    tiles, planes, side = volume.shape[0], volume.shape[1], volume.shape[-1]
    half = side // 2
    rows = transfer.shape[2]
    width = INTERSECTION
    parts = lax.axis_size("tile")
    table = trig_table(side)
    constants = jnp.asarray(np.concatenate([table, np.swapaxes(table, 1, 2)]))

    group = math.gcd(GROUP, planes)

    def spectra_of(tile, after, tables):
        return pl.pallas_call(
            functools.partial(spectra_kernel, tile=tile),
            out_shape=jax.ShapeDtypeStruct((planes, 4, half, half), f32),
            in_specs=[vmem()] * 3,
            out_specs=vmem(),
            scratch_shapes=[pltpu.VMEM((group, side, side), f32)],
            compiler_params=params(),
            cost_estimate=pl.CostEstimate(
                flops=30 * planes * side**3, bytes_accessed=8 * planes * side**2, transcendentals=0
            ),
            name=f"spectra{tile}",
        )(after, volume, tables)

    tables = constants
    half_block = jax.ShapeDtypeStruct((planes, 2, rows, half), f32)
    first_row = jax.ShapeDtypeStruct((planes, 2, 1, half), f32)
    lent = pl.pallas_call(
        functools.partial(lend_kernel, parts=parts),
        out_shape=half_block,
        in_specs=[pl.BlockSpec(memory_space=pl.ANY)],
        out_specs=vmem(),
        scratch_shapes=[pltpu.VMEM((planes, 2, rows, half), f32), pltpu.SemaphoreType.DMA((2,))],
        compiler_params=params(),
        cost_estimate=pl.CostEstimate(flops=LEND_COST, bytes_accessed=8 * planes * rows * side, transcendentals=0),
        name="lend",
    )(transfer)
    recv = lax.ppermute(lent, "tile", [(i, parts - 1 - i) for i in range(parts)])
    early = [spectra_of(0, lent, tables)]
    lent_first = pl.pallas_call(
        first_kernel, out_shape=first_row, in_specs=[vmem()] * 2, out_specs=vmem(), compiler_params=params(), name="first"
    )(lent, early[0] if FIRST_LATE else lent)
    recv_first = lax.ppermute(lent_first, "tile", [(i, (parts - i) % parts) for i in range(parts)])
    own, rotor = pl.pallas_call(
        functools.partial(arrange_kernel, parts=parts),
        out_shape=(half_block, jax.ShapeDtypeStruct((3, planes, half), f32)),
        in_specs=[pl.BlockSpec(memory_space=pltpu.SMEM), vmem(), vmem()],
        out_specs=(vmem(), vmem()),
        compiler_params=params(),
        name="arrange",
    )(phases, lent_first, transfer)
    recv, early[0], own = lax.optimization_barrier((recv, early[0], own))
    block = pl.pallas_call(
        functools.partial(pair_kernel, parts=parts),
        out_shape=half_block,
        in_specs=[vmem()] * 4,
        out_specs=vmem(),
        compiler_params=params(),
        name="pair",
    )(own, rotor, recv, recv_first)
    held = first_round(block, parts)
    spectra = early + [spectra_of(t, block, tables) for t in range(1, tiles)]
    sources = [mask for mask in held if mask]
    tied = lax.optimization_barrier(tuple(held[mask] for mask in sources) + tuple(spectra))
    if TIE_SPECTRA:
        held.update(zip(sources, tied))
        spectra = list(tied[len(sources) :])
    if NEAR_FIRST:
        near = both_cores(held)
    more = second_round(held, parts)
    if not NEAR_FIRST:
        near = both_cores(held)

    def project(blocks, masks_in, apart, name):
        count = len(masks_in)
        if apart:
            shapes = (jax.ShapeDtypeStruct((count, 2, rows, half), f32),) * tiles
        else:
            shapes = (jax.ShapeDtypeStruct((tiles, count, 2, rows, half), f32),)
        return pl.pallas_call(
            functools.partial(project_kernel, masks_in=masks_in, parts=parts, tiles=tiles, apart=apart),
            out_shape=shapes,
            in_specs=[vmem()] * (count + tiles),
            out_specs=(vmem(),) * len(shapes),
            compiler_params=params(),
            name=name,
        )(*[blocks[mask] for mask in masks_in], *spectra)

    near_masks = tuple(sorted(near))
    near_own, near_received = depth_sum(list(project(near, near_masks, False, "project_near")))
    order = list(more)
    if FAR_EACH:
        tied = [lax.optimization_barrier((more[mask], near_own[0]))[0] for mask in order]
    else:
        tied = lax.optimization_barrier(tuple(more[mask] for mask in order) + (near_own[0],))[:-1]
    far = both_cores(dict(zip(order, tied)))
    mask_sets = (near_masks, tuple(sorted(far)))
    far_masks = list(far)
    tied = lax.optimization_barrier(tuple(far[mask] for mask in far_masks) + (near_received[0],))
    far = dict(zip(far_masks, tied[:-1]))
    near_received = [tied[-1]]
    blocks = {**near, **far}
    factor, weights = pl.pallas_call(
        functools.partial(assemble_kernel, parts=parts, tiles=tiles),
        out_shape=(
            jax.ShapeDtypeStruct((planes, 4, half, half), f32),
            jax.ShapeDtypeStruct((tiles + 1, width, side), f32),
        ),
        in_specs=[pl.BlockSpec(memory_space=pltpu.SMEM)] + [vmem()] * parts,
        out_specs=(vmem(), vmem()),
        compiler_params=params(),
        name="assemble",
    )(margins, *[blocks[mask] for mask in range(parts)])

    far_sums = list(project(far, mask_sets[1], True, "project_far"))
    for t in range(1, tiles):
        if TIE_FAR:
            far_sums[t] = lax.optimization_barrier((far_sums[t], weights))[0]
    far_own, far_received = depth_sum(far_sums)

    backward = [((i + 1) % parts, i) for i in range(parts)]
    forward = [(i, (i + 1) % parts) for i in range(parts)]

    tops, bottoms = [[] for _ in range(tiles + 1)], [[] for _ in range(tiles + 1)]
    pieces = []
    for t in range(tiles):
        last = t == tiles - 1
        cuts = [0, *(planes * cut // 8 for cut in CUTS), planes] if last and planes % 8 == 0 else [0, planes]
        spectrum = None
        for begin, end in zip(cuts[:-1], cuts[1:]):
            step = math.gcd(GROUP, end - begin)
            if spectrum is None:
                inputs = [near_own[0], far_own[t], near_received[0], far_received[t], background, measured]
            else:
                inputs = [spectrum]
            inputs += [factor, volume, tables]
            edge = jax.ShapeDtypeStruct((end - begin, width, side), f32)
            updated, top, bottom, made = pl.pallas_call(
                functools.partial(update_kernel, tile=t, begin=begin, end=end, mask_sets=mask_sets, parts=parts),
                out_shape=(
                    jax.ShapeDtypeStruct((end - begin, side, side), f32), edge, edge,
                    jax.ShapeDtypeStruct((4, half, half) if spectrum is None else (8, 128), f32),
                ),
                in_specs=[vmem()] * len(inputs),
                out_specs=(vmem(),) * 4,
                scratch_shapes=[pltpu.VMEM((step, side, side), f32)],
                compiler_params=params(),
                cost_estimate=pl.CostEstimate(
                    flops=(40 if t == 0 else LATER_COST) * (end - begin) * side**3,
                    bytes_accessed=(12 if t == 0 else LATER_COST) * (end - begin) * side**2,
                    transcendentals=0,
                ),
                name=f"update{t}_{begin}",
            )(*inputs)
            cut = (begin, end)
            if spectrum is None:
                spectrum = made
            pieces.append((updated, t, cut))
            tops[t].append((top, cut))
            bottoms[t + 1].append((bottom, cut))
            if t == 0:
                tops[tiles].append((lax.ppermute(top, "tile", backward), cut))
            if last:
                bottoms[0].append((lax.ppermute(bottom, "tile", forward), cut))
                if begin < cuts[-2] == end and TIE_TOP:
                    tied = lax.optimization_barrier((spectrum, tops[tiles][0][0]))
                    spectrum, tops[tiles][0] = tied[0], (tied[1], tops[tiles][0][1])

    result = None
    for places in (tuple(range(1, tiles + 1)), (0,)):
        edges = [x for sides in (tops, bottoms) for j in places for x, _ in sides[j]]
        made = pieces if result is None else []
        inputs = [weights] + edges + [x for x, _, _ in made]
        aliased = int(result is not None)
        result = pl.pallas_call(
            functools.partial(
                blend_kernel,
                places=places,
                tiles=tiles,
                top_cuts={j: [cut for _, cut in tops[j]] for j in places},
                bottom_cuts={j: [cut for _, cut in bottoms[j]] for j in places},
                made=[(tile, cut) for _, tile, cut in made],
                aliased=aliased,
            ),
            out_shape=jax.ShapeDtypeStruct(volume.shape, f32),
            in_specs=[vmem()] * len(inputs) + [pl.BlockSpec(memory_space=pl.ANY)] * aliased,
            out_specs=pl.BlockSpec(memory_space=pl.ANY),
            scratch_shapes=[
                pltpu.VMEM((len(places), planes, width, side), f32),
                pltpu.SemaphoreType.DMA((2 * len(places) + len(made),)),
            ],
            input_output_aliases={len(inputs): 0} if aliased else {},
            compiler_params=params(),
            name=f"blend{places[0]}",
        )(*inputs, *([result] if aliased else []))
    return result


def solution(mesh):
    return jax.shard_map(
        on_device,
        mesh=mesh,
        in_specs=(
            P("tile", "depth", None, None),
            P("depth", None, "tile", None),
            P("tile", None, None),
            P("tile", None, None),
            P(),
            P("depth"),
        ),
        out_specs=P("tile", "depth", None, None),
        check_vma=False,
    )
```
